512 devices in a mesh: row: 64 (over y, z), col: 8 (over x, core).
Axes of the slice: x: 4, y: 8, z: 8, core: 2. Of those that a mesh axis runs over, the one named last changes fastest.
Arguments:
- hidden: bfloat16 [98304, 7168], P('row', 'col'), may hold values from -60 to 60, as said below
- test_matrix: bfloat16 [7168, 256], P('col'), may hold values from -6 to 6
Outputs:
- basis: float32 [98304, 256], P(('row', 'col'))
- factor: float32 [256, 256], replicated
The draws below stay inside these ranges and needn't reach their ends.
Inputs may be any that keep to these rules, and one draw needn't show every extreme that they name: `hidden`: hidden states of 98304 tokens.
All inputs are finite; a program needn't handle non-finite values.
Results may differ from the reference program's by a relative error of at most 0.003.
Values may be sent and summed in bfloat16 or wider, within the bound.
No kernel may reach another device: no remote copies, remote signals or barrier semaphores. Data moves between devices by JAX's collectives and lax.ppermute only.
A program may use at most 64 MiB of HBM per device.

```python
import math
import jax
import jax.numpy as jnp
from jax import lax

D = 7168
K = 256
TOKENS = 98304


def draw_hidden(key, part):
    key = jax.random.fold_in(key, 11)
    noise_key, scale_key = jax.random.split(key)
    position = jnp.arange(TOKENS, dtype=jnp.float32)[:, None] / TOKENS
    noise = jnp.clip(jax.random.normal(noise_key, (TOKENS, D), jnp.float32), -6.0, 6.0)
    spread = jax.random.uniform(scale_key, (TOKENS, 1), jnp.float32, 0.0, math.log(3.0))
    row_scale = jnp.exp(spread) * (1.0 + 2.0 * position)
    return (noise * row_scale).astype(jnp.bfloat16)


def level_of(own_key, shape, pieces, least, high):
    factor_of = 1.0
    for dim, parts in pieces:
        draws = jax.random.uniform(jax.random.fold_in(jax.random.fold_in(own_key, 6), dim), (parts,), jnp.float32, least / len(pieces), high / len(pieces))
        factor_of = factor_of * jnp.repeat(jnp.exp(draws), shape[dim] // parts).reshape((-1,) + (1,) * (len(shape) - 1 - dim))
    return factor_of


def bell_draw(key, dims, deviation, bound, pieces=(), kind=jnp.bfloat16):
    factor_of = level_of(key, dims, pieces, -0.22, 0.18) if pieces else 1.0
    array = jax.random.normal(key, dims, jnp.float32) * deviation * factor_of
    return jnp.minimum(jnp.maximum(array, -bound), bound).astype(kind)


def setup_inputs(seed: int = 0) -> dict:
    splits = jax.random.split(jax.random.key(seed), 3)
    hidden = draw_hidden(jax.random.fold_in(splits[2], 71), 0)
    test_matrix = bell_draw(splits[1], (D, K), 1.0, 6.0, ((0, 8),))
    return {"hidden": hidden, "test_matrix": test_matrix}


def reference(hidden, test_matrix):
    first = (jnp.dot(hidden.astype(jnp.float32), test_matrix.astype(jnp.float32), preferred_element_type=jnp.float32) * (1.0 / math.sqrt(D))).astype(jnp.bfloat16)
    back = (jnp.dot(hidden.T.astype(jnp.float32), first.astype(jnp.float32), preferred_element_type=jnp.float32) * (1.0 / TOKENS)).astype(jnp.bfloat16)
    sketch = jnp.dot(hidden.astype(jnp.float32), back.astype(jnp.float32), preferred_element_type=jnp.float32)
    ortho, factor = jnp.linalg.qr(sketch * (1.0 / math.sqrt(TOKENS)))
    diag_signs = jnp.where(jnp.diagonal(factor) < 0, -1.0, 1.0).astype(factor.dtype)
    factor = factor * diag_signs[:, None]
    basis = lax.linalg.triangular_solve(factor, sketch.T, left_side=True, lower=False, transpose_a=True).T
    return (basis, factor)
```

```python
import math

import jax
import jax.numpy as jnp
from jax import lax
from jax.experimental import pallas as pl
from jax.experimental.pallas import tpu as pltpu
from jax.sharding import Mesh, PartitionSpec as P

D = 7168
K = 256
HIGH = lax.Precision.HIGHEST

def mm(a, b):
    return jnp.dot(a, b, precision=HIGH, preferred_element_type=jnp.float32)

def mtm(a, b):
    return lax.dot_general(a, b, (((0,), (0,)), ((), ())), precision=HIGH, preferred_element_type=jnp.float32)

def low(a, b):
    return jnp.dot(a.astype(jnp.bfloat16), b.astype(jnp.bfloat16), preferred_element_type=jnp.float32)

def low_tm(a, b):
    return lax.dot_general(a.astype(jnp.bfloat16), b.astype(jnp.bfloat16), (((0,), (0,)), ((), ())), preferred_element_type=jnp.float32)


def factor_kernel(gram_ref, rows_ref, basis_ref, factor_ref, g_ref, x_ref, work_ref):
    row = lax.broadcasted_iota(jnp.int32, (K, K), 0)
    col = lax.broadcasted_iota(jnp.int32, (K, K), 1)
    eye = (row == col).astype(jnp.float32)
    upper = jnp.where(row < col, 1.0, jnp.where(row == col, 0.5, 0.0))
    gram = gram_ref[...]
    on_diag = jnp.where(row == col, gram, 0.0)
    s_row = lax.rsqrt(jnp.sum(on_diag, axis=0, keepdims=True))
    s_col = lax.rsqrt(jnp.sum(on_diag, axis=1, keepdims=True))
    g_ref[...] = gram * s_row * s_col
    x_ref[...] = eye * s_row

    def size(e):
        return jnp.sum(e * e)

    def step(state):
        count, _ = state
        g = g_ref[...]
        f = (g - eye) * upper
        a = f - low_tm(f, f) * upper
        t = eye - a + low(a, a)
        new = mtm(t, mm(g, t))
        g_ref[...] = new
        x_ref[...] = mm(x_ref[...], t)
        return count + 1, size(new - eye)

    def more(state):
        count, err = state
        return jnp.logical_and(count < 12, err > 1e-5)

    _, err = lax.while_loop(more, step, (jnp.int32(0), size(g_ref[...] - eye)))
    ok = err <= 1e-5

    @pl.when(ok)
    def _():
        x_ref[...] = mm(x_ref[...], eye - (g_ref[...] - eye) * upper)

    @pl.when(jnp.logical_not(ok))
    def _():
        work_ref[:, :K] = gram
        work_ref[:, K:] = eye
        lane = lax.broadcasted_iota(jnp.int32, (1, 2 * K), 1)

        def eliminate(k, carry):
            line = work_ref[pl.ds(k, 1), :]
            pivot = jnp.sum(jnp.where(lane == k, line, 0.0), axis=1, keepdims=True)
            line = line * lax.rsqrt(pivot)
            coef = jnp.where(lane[:, :K] > k, line[:, :K], 0.0)
            outer = lax.dot_general(coef, line, (((0,), (0,)), ((), ())), precision=HIGH, preferred_element_type=jnp.float32)
            work_ref[...] = work_ref[...] - outer
            work_ref[pl.ds(k, 1), :] = line
            return carry

        lax.fori_loop(0, K, eliminate, 0)
        x_ref[...] = work_ref[:, K:].T

    x = jnp.where(row <= col, x_ref[...], 0.0)
    factor_ref[...] = jnp.where(row <= col, mtm(x, gram), 0.0)
    basis_ref[...] = mm(rows_ref[...], x)


def factor_call(gram, rows):
    n = rows.shape[0]
    return pl.pallas_call(
        factor_kernel,
        out_shape=(jax.ShapeDtypeStruct((n, K), jnp.float32), jax.ShapeDtypeStruct((K, K), jnp.float32)),
        in_specs=[pl.BlockSpec(memory_space=pltpu.VMEM)] * 2,
        out_specs=(pl.BlockSpec(memory_space=pltpu.VMEM),) * 2,
        scratch_shapes=[pltpu.VMEM((K, K), jnp.float32), pltpu.VMEM((K, K), jnp.float32), pltpu.VMEM((K, 2 * K), jnp.float32)],
        compiler_params=pltpu.CompilerParams(vmem_limit_bytes=32 * 1024 * 1024),
    )(gram, rows)


ROW = ("y", "z")
COL = ("x", "core")


def scattered_sum(block, axis, dtype):
    count = lax.axis_size(axis)
    pieces = block.astype(dtype).reshape(count, block.shape[0] // count, K)
    return jnp.sum(lax.all_to_all(pieces, axis, 0, 0).astype(jnp.float32), axis=0)


def gathered(block, axis):
    count = lax.axis_size(axis)
    return lax.all_to_all(jnp.broadcast_to(block[None], (count, *block.shape)), axis, 0, 0)


def gathered_sum(block, axis, dtype):
    return jnp.sum(gathered(block.astype(dtype), axis).astype(jnp.float32), axis=0)


def body(hidden, test_matrix):
    tok_rows, width = hidden.shape
    total_rows = tok_rows * lax.axis_size(ROW)
    partial_first = jnp.dot(hidden, test_matrix, preferred_element_type=jnp.float32)
    my_first = (scattered_sum(partial_first, COL, jnp.bfloat16) * (1.0 / math.sqrt(D))).astype(jnp.bfloat16)
    first = gathered(my_first, COL).reshape(tok_rows, K)
    local_back = lax.dot_general(
        hidden, first, (((0,), (0,)), ((), ())), preferred_element_type=jnp.float32
    )
    my_back = scattered_sum(local_back, "z", jnp.bfloat16)
    my_back = (gathered_sum(my_back, "y", jnp.bfloat16) * (1.0 / total_rows)).astype(jnp.bfloat16)
    back = gathered(my_back, "z").reshape(width, K)
    partial_sketch = jnp.dot(hidden, back, preferred_element_type=jnp.float32)
    my_rows = scattered_sum(partial_sketch, COL, jnp.bfloat16)
    my_gram = jnp.dot(
        my_rows.T, my_rows, precision=lax.Precision.HIGHEST, preferred_element_type=jnp.float32
    )
    my_gram = scattered_sum(my_gram * (1.0 / total_rows), COL, jnp.float32)
    my_gram = gathered_sum(my_gram, "z", jnp.float32)
    my_gram = gathered_sum(my_gram, "y", jnp.float32)
    gram = gathered(my_gram, COL).reshape(K, K)
    return factor_call(gram, my_rows)


def solution(mesh):
    rows, cols = mesh.devices.shape
    side = math.isqrt(rows)
    grid = Mesh(mesh.devices.reshape(side, rows // side, cols // 2, 2), (*ROW, *COL))
    in_specs = (P(ROW, COL), P(COL, None))
    out_specs = (P((*ROW, *COL), None), P())
    return jax.shard_map(body, mesh=grid, in_specs=in_specs, out_specs=out_specs, check_vma=False)
```

```python
import math

import jax
import jax.numpy as jnp
from jax import lax
from jax.experimental import pallas as pl
from jax.experimental.pallas import tpu as pltpu
from jax.sharding import Mesh, PartitionSpec as P

D = 7168
K = 256
HALF = K // 2
HIGH = lax.Precision.HIGHEST

def mm(a, b):
    return jnp.dot(a, b, precision=HIGH, preferred_element_type=jnp.float32)

def mtm(a, b):
    return lax.dot_general(a, b, (((0,), (0,)), ((), ())), precision=HIGH, preferred_element_type=jnp.float32)

def low(a, b):
    return jnp.dot(a.astype(jnp.bfloat16), b.astype(jnp.bfloat16), preferred_element_type=jnp.float32)

def low_tm(a, b):
    return lax.dot_general(a.astype(jnp.bfloat16), b.astype(jnp.bfloat16), (((0,), (0,)), ((), ())), preferred_element_type=jnp.float32)


def factor_kernel(packed_ref, rows_ref, basis_ref, factor_ref, gram_ref, g_ref, x_ref, work_ref):
    corner = packed_ref[HALF : 2 * HALF, :]
    gram_ref[:HALF, :HALF] = packed_ref[:HALF, :]
    gram_ref[:HALF, HALF:] = corner
    gram_ref[HALF:, :HALF] = corner.T
    gram_ref[HALF:, HALF:] = packed_ref[2 * HALF :, :]
    row = lax.broadcasted_iota(jnp.int32, (K, K), 0)
    col = lax.broadcasted_iota(jnp.int32, (K, K), 1)
    eye = (row == col).astype(jnp.float32)
    upper = jnp.where(row < col, 1.0, jnp.where(row == col, 0.5, 0.0))
    gram = gram_ref[...]
    on_diag = jnp.where(row == col, gram, 0.0)
    s_row = lax.rsqrt(jnp.sum(on_diag, axis=0, keepdims=True))
    s_col = lax.rsqrt(jnp.sum(on_diag, axis=1, keepdims=True))
    g_ref[...] = gram * s_row * s_col
    x_ref[...] = eye * s_row

    def size(e):
        return jnp.sum(e * e)

    def step(state):
        count, _ = state
        g = g_ref[...]
        f = (g - eye) * upper
        a = f - low_tm(f, f) * upper
        t = eye - a + low(a, a)
        new = mtm(t, mm(g, t))
        g_ref[...] = new
        x_ref[...] = mm(x_ref[...], t)
        return count + 1, size(new - eye)

    def more(state):
        count, err = state
        return jnp.logical_and(count < 12, err > 1e-5)

    _, err = lax.while_loop(more, step, (jnp.int32(0), size(g_ref[...] - eye)))
    ok = err <= 1e-5

    @pl.when(ok)
    def _():
        x_ref[...] = mm(x_ref[...], eye - (g_ref[...] - eye) * upper)

    @pl.when(jnp.logical_not(ok))
    def _():
        work_ref[:, :K] = gram
        work_ref[:, K:] = eye
        lane = lax.broadcasted_iota(jnp.int32, (1, 2 * K), 1)

        def eliminate(k, carry):
            line = work_ref[pl.ds(k, 1), :]
            pivot = jnp.sum(jnp.where(lane == k, line, 0.0), axis=1, keepdims=True)
            line = line * lax.rsqrt(pivot)
            coef = jnp.where(lane[:, :K] > k, line[:, :K], 0.0)
            outer = lax.dot_general(coef, line, (((0,), (0,)), ((), ())), precision=HIGH, preferred_element_type=jnp.float32)
            work_ref[...] = work_ref[...] - outer
            work_ref[pl.ds(k, 1), :] = line
            return carry

        lax.fori_loop(0, K, eliminate, 0)
        x_ref[...] = work_ref[:, K:].T

    x = jnp.where(row <= col, x_ref[...], 0.0)
    factor_ref[...] = jnp.where(row <= col, mtm(x, gram), 0.0)
    basis_ref[...] = mm(rows_ref[...], x)


def factor_call(packed, rows):
    square = pltpu.VMEM((K, K), jnp.float32)
    return pl.pallas_call(
        factor_kernel,
        out_shape=(jax.ShapeDtypeStruct(rows.shape, jnp.float32), jax.ShapeDtypeStruct((K, K), jnp.float32)),
        in_specs=[WHOLE] * 2,
        out_specs=(WHOLE, WHOLE),
        scratch_shapes=[square, square, square, pltpu.VMEM((K, 2 * K), jnp.float32)],
        compiler_params=PARAMS,
        name="factor",
    )(packed, rows)


WHOLE = pl.BlockSpec(memory_space=pltpu.VMEM)
PARAMS = pltpu.CompilerParams(vmem_limit_bytes=32 * 1024 * 1024)


def rows_kernel(over_rows, which_ref, left_ref, right_ref, out_ref):
    dims = (((1,), (0 if over_rows else 1,)), ((), ()))
    out_ref[...] = lax.dot_general(left_ref[...], right_ref[...], dims, preferred_element_type=jnp.float32)


def half_product(hidden, right, half, over_rows):
    rows, width = hidden.shape
    tile = rows // 8
    spec = pltpu.PrefetchScalarGridSpec(
        num_scalar_prefetch=1,
        grid=(4,),
        in_specs=[
            pl.BlockSpec((tile, width), lambda i, which: (2 * i + which[0], 0)),
            pl.BlockSpec(right.shape, lambda i, which: (0, 0)),
        ],
        out_specs=pl.BlockSpec((tile, K), lambda i, which: (i, 0)),
    )
    return pl.pallas_call(
        lambda *refs: rows_kernel(over_rows, *refs),
        out_shape=jax.ShapeDtypeStruct((rows // 2, K), jnp.float32),
        grid_spec=spec,
        compiler_params=PARAMS,
        name="half_product",
    )(half, hidden, right)


def back_kernel(which_ref, first_ref, hidden_ref, out_ref):
    part = lax.dot_general(first_ref[...], hidden_ref[...], (((0,), (0,)), ((), ())), preferred_element_type=jnp.float32)

    @pl.when(pl.program_id(0) == 0)
    def _():
        out_ref[...] = part

    @pl.when(pl.program_id(0) > 0)
    def _():
        out_ref[...] = out_ref[...] + part


def half_back(hidden, first, half):
    rows, width = hidden.shape
    tile = rows // 8
    spec = pltpu.PrefetchScalarGridSpec(
        num_scalar_prefetch=1,
        grid=(4,),
        in_specs=[
            pl.BlockSpec((tile, K), lambda i, which: (i, 0)),
            pl.BlockSpec((tile, width), lambda i, which: (2 * i + which[0], 0)),
        ],
        out_specs=pl.BlockSpec((K, width), lambda i, which: (0, 0)),
    )
    return pl.pallas_call(
        back_kernel,
        out_shape=jax.ShapeDtypeStruct((K, width), jnp.float32),
        grid_spec=spec,
        compiler_params=PARAMS,
        name="half_back",
    )(half, first, hidden)


def gram_kernel(rows_ref, packed_ref):
    left, right = rows_ref[:, :HALF], rows_ref[:, HALF:]
    packed_ref[:HALF, :] = mtm(left, left)
    packed_ref[HALF : 2 * HALF, :] = mtm(left, right)
    packed_ref[2 * HALF :, :] = mtm(right, right)


def packed_gram(rows):
    return pl.pallas_call(
        gram_kernel,
        out_shape=jax.ShapeDtypeStruct((3 * HALF, HALF), jnp.float32),
        in_specs=[WHOLE],
        out_specs=WHOLE,
        compiler_params=PARAMS,
        name="packed_gram",
    )(rows)


ROW = ("y", "z")
COL = ("x", "core")
ALL = (*ROW, *COL)


def swapped(block):
    return lax.ppermute(block, "core", [(0, 1), (1, 0)])


def line_groups(sizes, along):
    ys, zs, xs = sizes
    groups = []
    for core in range(2):
        y_steps, z_steps = along[core]
        for y in range(ys):
            for z in range(zs):
                if any(y // s % n for s, n in y_steps) or any(z // s % n for s, n in z_steps):
                    continue
                spots = [(y, z)]
                for s, n in y_steps:
                    spots = [(a + s * k, b) for a, b in spots for k in range(n)]
                for s, n in z_steps:
                    spots = [(a, b + s * k) for a, b in spots for k in range(n)]
                for x in range(xs):
                    groups.append([((a * zs + b) * xs + x) * 2 + core for a, b in spots])
    return groups


def exchanged(pieces, axis, groups=None):
    return lax.all_to_all(pieces, axis, 0, 0, axis_index_groups=groups)


def spread(block, count):
    return jnp.broadcast_to(block[None], (count, *block.shape))


def total(pieces):
    return jnp.sum(pieces.astype(jnp.float32), axis=0)


def body(sizes, hidden, test_matrix):
    bf16 = jnp.bfloat16
    tok_rows, width = hidden.shape
    tile = tok_rows // 8
    ys, zs, xs = sizes
    total_rows = tok_rows * ys * zs
    core = lax.axis_index("core")
    mine, other = core.reshape(1), (1 - core).reshape(1)

    landed = swapped(half_product(hidden, test_matrix, other, True))
    pieces = (half_product(hidden, test_matrix, mine, True) + landed).astype(bf16).reshape(xs, tile, K)
    my_first = (total(exchanged(pieces, "x")) * (1.0 / math.sqrt(D))).astype(bf16)
    my_half = exchanged(spread(my_first, xs), "x").reshape(tok_rows // 2, K)
    other_half = swapped(my_half)
    local_back = half_back(hidden, my_half, mine) + half_back(hidden, other_half, other)

    wide = line_groups(sizes, ((((1, 2),), ((1, zs),)), (((1, ys),), ((1, 2),))))
    rest = line_groups(sizes, ((((2, ys // 2),), ()), ((), ((2, zs // 2),))))
    n_wide, n_rest = len(wide[0]), len(rest[0])
    pieces = local_back.astype(bf16).reshape(n_wide, K // n_wide, width)
    my_back = total(exchanged(pieces, ALL, wide))
    my_back = total(exchanged(spread(my_back, n_rest), ALL, rest))
    my_back = (my_back * (1.0 / total_rows)).astype(bf16)
    back = exchanged(spread(my_back, n_wide), ALL, wide).reshape(K, width)

    landed = swapped(half_product(hidden, back, other, False))
    own = half_product(hidden, back, mine, False) + landed
    pieces = own.reshape(xs, tile, K)
    landed = exchanged(pieces.astype(bf16), "x").astype(jnp.float32)
    mine_of_x = lax.broadcasted_iota(jnp.int32, (xs, 1, 1), 0) == lax.axis_index("x")
    my_rows = jnp.sum(jnp.where(mine_of_x, pieces, landed), axis=0)

    gram = packed_gram(my_rows) * (1.0 / total_rows)
    gram = total(exchanged(gram.reshape(8, 3 * HALF // 8, HALF), COL))
    lines = [((), ((1, zs),)), (((1, ys),), ())]
    for along in (lines, lines[::-1]):
        groups = line_groups(sizes, along)
        gram = total(exchanged(spread(gram, len(groups[0])), ALL, groups))
    gram = exchanged(spread(gram, 8), COL).reshape(3 * HALF, HALF)
    return factor_call(gram, my_rows)


def solution(mesh):
    rows, cols = mesh.devices.shape
    side = math.isqrt(rows)
    sizes = (side, rows // side, cols // 2)
    grid = Mesh(mesh.devices.reshape(*sizes, 2), ALL)
    in_specs = (P(ROW, COL), P(COL, None))
    out_specs = (P(ALL, None), P())
    return jax.shard_map(
        lambda *args: body(sizes, *args), mesh=grid, in_specs=in_specs, out_specs=out_specs, check_vma=False
    )
```

```python
import math

import jax
import jax.numpy as jnp
from jax import lax
from jax.experimental import pallas as pl
from jax.experimental.pallas import tpu as pltpu
from jax.sharding import Mesh, PartitionSpec as P

D = 7168
K = 256
HALF = K // 2
HIGH = lax.Precision.HIGHEST

def dot(a, b, over_a=1, over_b=0, precision=None):
    return lax.dot_general(
        a, b, (((over_a,), (over_b,)), ((), ())), precision=precision, preferred_element_type=jnp.float32
    )


def terms(a, count):
    parts = []
    for _ in range(count):
        parts.append(a.astype(jnp.bfloat16))
        a = a - parts[-1].astype(jnp.float32)
    return parts


def factor_kernel(packed_ref, rows_ref, basis_ref, factor_ref, gram_ref, g_ref, x_ref, work_ref):
    bf16 = jnp.bfloat16
    corner = packed_ref[HALF : 2 * HALF, :]
    gram_ref[:HALF, :HALF] = packed_ref[:HALF, :]
    gram_ref[:HALF, HALF:] = corner
    gram_ref[HALF:, :HALF] = corner.T
    gram_ref[HALF:, HALF:] = packed_ref[2 * HALF :, :]
    row = lax.broadcasted_iota(jnp.int32, (K, K), 0)
    col = lax.broadcasted_iota(jnp.int32, (K, K), 1)
    eye = (row == col).astype(jnp.float32)
    upper = jnp.where(row < col, 1.0, jnp.where(row == col, 0.5, 0.0))
    on_diag = jnp.where(row == col, gram_ref[...], 0.0)
    s_row = lax.rsqrt(jnp.sum(on_diag, axis=0, keepdims=True))
    s_col = lax.rsqrt(jnp.sum(on_diag, axis=1, keepdims=True))

    def change_for(g):
        f = (g - eye) * upper
        fb = f.astype(bf16)
        a = f - dot(fb, fb, 0, 0) * upper
        ab = a.astype(bf16)
        return (dot(ab, ab) - a).astype(bf16)

    def moved(g, n):
        y = g + sum(dot(part, n) for part in terms(g, 3))
        return y + sum(dot(n, part, 0, 0) for part in terms(y, 3))

    def size(e):
        return jnp.sum(e * e)

    g = gram_ref[...] * s_row * s_col
    n = change_for(g)
    x_ref[...] = s_col * (eye + n.astype(jnp.float32))
    g_ref[...] = moved(g, n)

    def step(state):
        count, _ = state
        g = g_ref[...]
        n = change_for(g)
        g = moved(g, n)
        g_ref[...] = g
        x = x_ref[...]
        x_ref[...] = x + sum(dot(part, n) for part in terms(x, 3))
        return count + 1, size(g - eye)

    def more(state):
        count, err = state
        return jnp.logical_and(count < 12, err > 1e-5)

    _, err = lax.while_loop(more, step, (jnp.int32(0), jnp.float32(1.0)))
    ok = err <= 1e-5

    @pl.when(ok)
    def _():
        x = x_ref[...]
        last = ((g_ref[...] - eye) * upper).astype(bf16)
        x_ref[...] = x - sum(dot(part, last) for part in terms(x, 2))

    @pl.when(jnp.logical_not(ok))
    def _():
        work_ref[:, :K] = gram_ref[...]
        work_ref[:, K:] = eye
        lane = lax.broadcasted_iota(jnp.int32, (1, 2 * K), 1)

        def eliminate(k, carry):
            line = work_ref[pl.ds(k, 1), :]
            pivot = jnp.sum(jnp.where(lane == k, line, 0.0), axis=1, keepdims=True)
            line = line * lax.rsqrt(pivot)
            coef = jnp.where(lane[:, :K] > k, line[:, :K], 0.0)
            work_ref[...] = work_ref[...] - dot(coef, line, 0, 0, HIGH)
            work_ref[pl.ds(k, 1), :] = line
            return carry

        lax.fori_loop(0, K, eliminate, 0)
        x_ref[...] = work_ref[:, K:].T

    x = jnp.where(row <= col, x_ref[...], 0.0)
    basis_ref[...] = dot(rows_ref[...], x, precision=HIGH)
    factor_ref[...] = jnp.where(row <= col, dot(x, gram_ref[...], 0, 0, HIGH), 0.0)


def factor_call(packed, rows):
    square = pltpu.VMEM((K, K), jnp.float32)
    return pl.pallas_call(
        factor_kernel,
        out_shape=(jax.ShapeDtypeStruct(rows.shape, jnp.float32), jax.ShapeDtypeStruct((K, K), jnp.float32)),
        in_specs=[WHOLE] * 2,
        out_specs=(WHOLE, WHOLE),
        scratch_shapes=[square, square, square, pltpu.VMEM((K, 2 * K), jnp.float32)],
        compiler_params=PARAMS,
        name="factor",
    )(packed, rows)


WHOLE = pl.BlockSpec(memory_space=pltpu.VMEM)
PARAMS = pltpu.CompilerParams(vmem_limit_bytes=32 * 1024 * 1024)


def streamed_kernel(which_ref, left_ref, right_ref, out_ref):
    out_ref[...] = dot(left_ref[...], right_ref[...])


def streamed_half(hidden, right, half):
    rows, width = hidden.shape
    steps = 2
    tile = rows // 2 // steps
    spec = pltpu.PrefetchScalarGridSpec(
        num_scalar_prefetch=1,
        grid=(steps,),
        in_specs=[
            pl.BlockSpec((tile, width), lambda i, which: (steps * which[0] + i, 0)),
            pl.BlockSpec(right.shape, lambda i, which: (0, 0)),
        ],
        out_specs=pl.BlockSpec((tile, K), lambda i, which: (i, 0)),
    )
    return pl.pallas_call(
        streamed_kernel,
        out_shape=jax.ShapeDtypeStruct((rows // 2, K), jnp.float32),
        grid_spec=spec,
        compiler_params=pltpu.CompilerParams(vmem_limit_bytes=56 * 1024 * 1024),
        name="streamed_half",
    )(half, hidden, right)


SCALAR = pl.BlockSpec(memory_space=pltpu.SMEM)


def half_kernel(which_ref, hidden_ref, right_ref, out_ref):
    rows = out_ref.shape[0]
    out_ref[...] = dot(hidden_ref[pl.ds(pl.multiple_of(which_ref[0] * rows, rows), rows), :], right_ref[...])


def striped_kernel(which_ref, hidden_ref, back_ref, out_ref):
    rows = out_ref.shape[0]
    tile = rows // 4
    blocks = [hidden_ref[pl.ds(pl.multiple_of((2 * i + which_ref[0]) * tile, tile), tile), :] for i in range(4)]
    out_ref[...] = dot(jnp.concatenate(blocks, axis=0), back_ref[...], 1, 1)


def half_product(kernel, hidden, right, half):
    return pl.pallas_call(
        kernel,
        out_shape=jax.ShapeDtypeStruct((hidden.shape[0] // 2, K), jnp.float32),
        in_specs=[SCALAR, WHOLE, WHOLE],
        out_specs=WHOLE,
        compiler_params=PARAMS,
        name="half_product",
    )(half, hidden, right)


def back_kernel(which_ref, hidden_ref, first_ref, *refs):
    *so_far, out_ref = refs
    rows = first_ref.shape[0]
    part = dot(first_ref[...], hidden_ref[pl.ds(pl.multiple_of(which_ref[0] * rows, rows), rows), :], 0, 0)
    for ref in so_far:
        part = part + ref[...]
    out_ref[...] = part.astype(out_ref.dtype)


def half_back(hidden, first, half, dtype, *so_far):
    return pl.pallas_call(
        back_kernel,
        out_shape=jax.ShapeDtypeStruct((K, hidden.shape[1]), dtype),
        in_specs=[SCALAR, *[WHOLE] * (2 + len(so_far))],
        out_specs=WHOLE,
        compiler_params=PARAMS,
        name="half_back",
    )(half, hidden, first, *so_far)


def gram_kernel(scale, x_ref, landed_ref, kept_ref, other_ref, rows_ref, packed_ref):
    count, tile, _ = landed_ref.shape
    own = pl.ds(pl.multiple_of(x_ref[0] * tile, tile), tile)
    rows = kept_ref[own, :] + other_ref[own, :]
    for i in range(count):
        rows = rows + jnp.where(x_ref[0] == i, 0.0, landed_ref[i].astype(jnp.float32))
    rows_ref[...] = rows
    left, right = rows[:, :HALF], rows[:, HALF:]
    packed_ref[:HALF, :] = dot(left, left, 0, 0, HIGH) * scale
    packed_ref[HALF : 2 * HALF, :] = dot(left, right, 0, 0, HIGH) * scale
    packed_ref[2 * HALF :, :] = dot(right, right, 0, 0, HIGH) * scale


def rows_and_gram(x, landed, kept, other, scale):
    return pl.pallas_call(
        lambda *refs: gram_kernel(scale, *refs),
        out_shape=(
            jax.ShapeDtypeStruct(landed.shape[1:], jnp.float32),
            jax.ShapeDtypeStruct((3 * HALF, HALF), jnp.float32),
        ),
        in_specs=[SCALAR, WHOLE, WHOLE, WHOLE],
        out_specs=(WHOLE, WHOLE),
        compiler_params=PARAMS,
        name="rows_and_gram",
    )(x, landed, kept, other)


ROW = ("y", "z")
COL = ("x", "core")
ALL = (*ROW, *COL)


def swapped(block):
    return lax.ppermute(block, "core", [(0, 1), (1, 0)])


def line_groups(sizes, along):
    ys, zs, xs = sizes
    groups = []
    for core in range(2):
        y_steps, z_steps = along[core]
        for y in range(ys):
            for z in range(zs):
                if any(y // s % n for s, n in y_steps) or any(z // s % n for s, n in z_steps):
                    continue
                spots = [(y, z)]
                for s, n in y_steps:
                    spots = [(a + s * k, b) for a, b in spots for k in range(n)]
                for s, n in z_steps:
                    spots = [(a, b + s * k) for a, b in spots for k in range(n)]
                for x in range(xs):
                    groups.append([((a * zs + b) * xs + x) * 2 + core for a, b in spots])
    return groups


def exchanged(pieces, axis, groups=None):
    return lax.all_to_all(pieces, axis, 0, 0, axis_index_groups=groups)


def spread(block, count):
    return jnp.broadcast_to(block[None], (count, *block.shape))


def total(pieces):
    return jnp.sum(pieces.astype(jnp.float32), axis=0)


def body(sizes, hidden, test_matrix):
    bf16 = jnp.bfloat16
    tok_rows, width = hidden.shape
    tile = tok_rows // 8
    ys, zs, xs = sizes
    total_rows = tok_rows * ys * zs
    core = lax.axis_index("core")
    mine, other = core.reshape(1), (1 - core).reshape(1)

    landed = swapped(streamed_half(hidden, test_matrix, other))
    pieces = (half_product(half_kernel, hidden, test_matrix, mine) + landed).astype(bf16).reshape(xs, tile, K)
    my_first = (total(exchanged(pieces, "x")) * (1.0 / math.sqrt(D))).astype(bf16)
    my_half = exchanged(spread(my_first, xs), "x").reshape(tok_rows // 2, K)
    other_half = swapped(my_half)
    local_back = half_back(hidden, my_half, mine, jnp.float32)
    local_back = half_back(hidden, other_half, other, bf16, local_back)

    pieces = local_back.reshape(ys * zs, K // (ys * zs), width)
    my_back = (total(exchanged(pieces, ROW)) * (1.0 / total_rows)).astype(bf16)
    back = exchanged(spread(my_back, ys * zs), ROW).reshape(K, width)

    landed = swapped(half_product(striped_kernel, hidden, back, other))
    kept = half_product(striped_kernel, hidden, back, mine)
    pieces = exchanged((kept + landed).astype(bf16).reshape(xs, tile, K), "x")
    my_rows, gram = rows_and_gram(lax.axis_index("x").reshape(1), pieces, kept, landed, 1.0 / total_rows)
    gram = total(exchanged(gram.reshape(8, 3 * HALF // 8, HALF), COL))
    lines = [((), ((1, zs),)), (((1, ys),), ())]
    for along in (lines, lines[::-1]):
        groups = line_groups(sizes, along)
        gram = total(exchanged(spread(gram, len(groups[0])), ALL, groups))
    gram = exchanged(spread(gram, 8), COL).reshape(3 * HALF, HALF)
    return factor_call(gram, my_rows)


def solution(mesh):
    rows, cols = mesh.devices.shape
    side = math.isqrt(rows)
    sizes = (side, rows // side, cols // 2)
    grid = Mesh(mesh.devices.reshape(*sizes, 2), ALL)
    in_specs = (P(ROW, COL), P(COL, None))
    out_specs = (P(ALL, None), P())
    return jax.shard_map(
        lambda *args: body(sizes, *args), mesh=grid, in_specs=in_specs, out_specs=out_specs, check_vma=False
    )
```

```python
import math

import jax
import jax.numpy as jnp
from jax import lax
from jax.experimental import pallas as pl
from jax.experimental.pallas import tpu as pltpu
from jax.sharding import Mesh, PartitionSpec as P

D = 7168
K = 256
HALF = K // 2
HIGH = lax.Precision.HIGHEST

def dot(a, b, over_a=1, over_b=0, precision=None):
    return lax.dot_general(
        a, b, (((over_a,), (over_b,)), ((), ())), precision=precision, preferred_element_type=jnp.float32
    )


def terms(a, count):
    parts = []
    for _ in range(count):
        parts.append(a.astype(jnp.bfloat16))
        a = a - parts[-1].astype(jnp.float32)
    return parts


def factor_kernel(packed_ref, rows_ref, basis_ref, factor_ref, gram_ref, g_ref, x_ref, work_ref):
    bf16 = jnp.bfloat16
    corner = packed_ref[HALF : 2 * HALF, :]
    gram_ref[:HALF, :HALF] = packed_ref[:HALF, :]
    gram_ref[:HALF, HALF:] = corner
    gram_ref[HALF:, :HALF] = corner.T
    gram_ref[HALF:, HALF:] = packed_ref[2 * HALF :, :]
    row = lax.broadcasted_iota(jnp.int32, (K, K), 0)
    col = lax.broadcasted_iota(jnp.int32, (K, K), 1)
    eye = (row == col).astype(jnp.float32)
    upper = jnp.where(row < col, 1.0, jnp.where(row == col, 0.5, 0.0))
    on_diag = jnp.where(row == col, gram_ref[...], 0.0)
    s_row = lax.rsqrt(jnp.sum(on_diag, axis=0, keepdims=True))
    s_col = lax.rsqrt(jnp.sum(on_diag, axis=1, keepdims=True))

    def change_for(g):
        f = (g - eye) * upper
        fb = f.astype(bf16)
        a = f - dot(fb, fb, 0, 0) * upper
        ab = a.astype(bf16)
        return (dot(ab, ab) - a).astype(bf16)

    def moved(g, n):
        y = g + sum(dot(part, n) for part in terms(g, 3))
        return y + sum(dot(n, part, 0, 0) for part in terms(y, 3))

    def size(e):
        return jnp.sum(e * e)

    g = gram_ref[...] * s_row * s_col
    n = change_for(g)
    x_ref[...] = s_col * (eye + n.astype(jnp.float32))
    g_ref[...] = moved(g, n)

    def step(state):
        count, _ = state
        g = g_ref[...]
        n = change_for(g)
        g = moved(g, n)
        g_ref[...] = g
        x = x_ref[...]
        x_ref[...] = x + sum(dot(part, n) for part in terms(x, 3))
        return count + 1, size(g - eye)

    def more(state):
        count, err = state
        return jnp.logical_and(count < 12, err > 1e-5)

    _, err = lax.while_loop(more, step, (jnp.int32(0), jnp.float32(1.0)))
    ok = err <= 1e-5

    @pl.when(ok)
    def _():
        x = x_ref[...]
        last = ((g_ref[...] - eye) * upper).astype(bf16)
        x_ref[...] = x - sum(dot(part, last) for part in terms(x, 2))

    @pl.when(jnp.logical_not(ok))
    def _():
        work_ref[:, :K] = gram_ref[...]
        work_ref[:, K:] = eye
        lane = lax.broadcasted_iota(jnp.int32, (1, 2 * K), 1)

        def eliminate(k, carry):
            line = work_ref[pl.ds(k, 1), :]
            pivot = jnp.sum(jnp.where(lane == k, line, 0.0), axis=1, keepdims=True)
            line = line * lax.rsqrt(pivot)
            coef = jnp.where(lane[:, :K] > k, line[:, :K], 0.0)
            work_ref[...] = work_ref[...] - dot(coef, line, 0, 0, HIGH)
            work_ref[pl.ds(k, 1), :] = line
            return carry

        lax.fori_loop(0, K, eliminate, 0)
        x_ref[...] = work_ref[:, K:].T

    x = jnp.where(row <= col, x_ref[...], 0.0)
    basis_ref[...] = dot(rows_ref[...], x, precision=HIGH)
    factor_ref[...] = jnp.where(row <= col, dot(x, gram_ref[...], 0, 0, HIGH), 0.0)


def factor_call(packed, rows):
    square = pltpu.VMEM((K, K), jnp.float32)
    return pl.pallas_call(
        factor_kernel,
        out_shape=(jax.ShapeDtypeStruct(rows.shape, jnp.float32), jax.ShapeDtypeStruct((K, K), jnp.float32)),
        in_specs=[WHOLE] * 2,
        out_specs=(WHOLE, WHOLE),
        scratch_shapes=[square, square, square, pltpu.VMEM((K, 2 * K), jnp.float32)],
        compiler_params=PARAMS,
        name="factor",
    )(packed, rows)


WHOLE = pl.BlockSpec(memory_space=pltpu.VMEM)
PARAMS = pltpu.CompilerParams(vmem_limit_bytes=12 * 1024 * 1024)


def streamed_kernel(which_ref, left_ref, right_ref, out_ref, left_buf, right_buf, sems):
    rows = out_ref.shape[0]
    tile = rows // STEPS
    copies = [pltpu.make_async_copy(right_ref, right_buf, sems.at[STEPS])]
    for i in range(STEPS):
        start = pl.multiple_of(which_ref[0] * rows + i * tile, tile)
        copies.append(pltpu.make_async_copy(left_ref.at[pl.ds(start, tile), :], left_buf.at[i], sems.at[i]))
    for copy in copies:
        copy.start()
    copies[0].wait()
    for i in range(STEPS):
        copies[1 + i].wait()
        out_ref[i * tile : (i + 1) * tile, :] = dot(left_buf[i], right_buf[...])


def streamed_half(hidden, right, half):
    rows, width = hidden.shape
    in_hbm = pl.BlockSpec(memory_space=pltpu.HBM)
    return pl.pallas_call(
        streamed_kernel,
        out_shape=jax.ShapeDtypeStruct((rows // 2, K), jnp.float32),
        in_specs=[SCALAR, in_hbm, in_hbm],
        out_specs=WHOLE,
        scratch_shapes=[
            pltpu.VMEM((STEPS, rows // 2 // STEPS, width), hidden.dtype),
            pltpu.VMEM(right.shape, right.dtype),
            pltpu.SemaphoreType.DMA((STEPS + 1,)),
        ],
        compiler_params=pltpu.CompilerParams(vmem_limit_bytes=60 * 1024 * 1024),
        name="streamed_half",
    )(half, hidden, right)


STEPS = 2
SCALAR = pl.BlockSpec(memory_space=pltpu.SMEM)


def half_kernel(which_ref, hidden_ref, right_ref, out_ref):
    rows = out_ref.shape[0]
    out_ref[...] = dot(hidden_ref[pl.ds(pl.multiple_of(which_ref[0] * rows, rows), rows), :], right_ref[...])


def striped_kernel(which_ref, hidden_ref, back_ref, out_ref):
    rows = out_ref.shape[0]
    tile = rows // 4
    blocks = [hidden_ref[pl.ds(pl.multiple_of((2 * i + which_ref[0]) * tile, tile), tile), :] for i in range(4)]
    out_ref[...] = dot(jnp.concatenate(blocks, axis=0), back_ref[...], 1, 1)


def half_product(kernel, hidden, right, half):
    return pl.pallas_call(
        kernel,
        out_shape=jax.ShapeDtypeStruct((hidden.shape[0] // 2, K), jnp.float32),
        in_specs=[SCALAR, WHOLE, WHOLE],
        out_specs=WHOLE,
        compiler_params=PARAMS,
        name="half_product",
    )(half, hidden, right)


def back_kernel(which_ref, hidden_ref, first_ref, *refs):
    *so_far, out_ref = refs
    rows = first_ref.shape[0]
    part = dot(first_ref[...], hidden_ref[pl.ds(pl.multiple_of(which_ref[0] * rows, rows), rows), :], 0, 0)
    for ref in so_far:
        part = part + ref[...]
    out_ref[...] = part.astype(out_ref.dtype)


def half_back(hidden, first, half, dtype, *so_far):
    return pl.pallas_call(
        back_kernel,
        out_shape=jax.ShapeDtypeStruct((K, hidden.shape[1]), dtype),
        in_specs=[SCALAR, *[WHOLE] * (2 + len(so_far))],
        out_specs=WHOLE,
        compiler_params=PARAMS,
        name="half_back",
    )(half, hidden, first, *so_far)


def gram_kernel(scale, x_ref, landed_ref, kept_ref, other_ref, rows_ref, packed_ref):
    count, tile, _ = landed_ref.shape
    own = pl.ds(pl.multiple_of(x_ref[0] * tile, tile), tile)
    rows = kept_ref[own, :] + other_ref[own, :]
    for i in range(count):
        rows = rows + jnp.where(x_ref[0] == i, 0.0, landed_ref[i].astype(jnp.float32))
    rows_ref[...] = rows
    left, right = rows[:, :HALF], rows[:, HALF:]
    packed_ref[:HALF, :] = dot(left, left, 0, 0, HIGH) * scale
    packed_ref[HALF : 2 * HALF, :] = dot(left, right, 0, 0, HIGH) * scale
    packed_ref[2 * HALF :, :] = dot(right, right, 0, 0, HIGH) * scale


def rows_and_gram(x, landed, kept, other, scale):
    return pl.pallas_call(
        lambda *refs: gram_kernel(scale, *refs),
        out_shape=(
            jax.ShapeDtypeStruct(landed.shape[1:], jnp.float32),
            jax.ShapeDtypeStruct((3 * HALF, HALF), jnp.float32),
        ),
        in_specs=[SCALAR, WHOLE, WHOLE, WHOLE],
        out_specs=(WHOLE, WHOLE),
        compiler_params=PARAMS,
        name="rows_and_gram",
    )(x, landed, kept, other)


ROW = ("y", "z")
COL = ("x", "core")
ALL = (*ROW, *COL)


def swapped(block):
    return lax.ppermute(block, "core", [(0, 1), (1, 0)])


def line_groups(sizes, along):
    ys, zs, xs = sizes
    groups = []
    for core in range(2):
        y_steps, z_steps = along[core]
        for y in range(ys):
            for z in range(zs):
                if any(y // s % n for s, n in y_steps) or any(z // s % n for s, n in z_steps):
                    continue
                spots = [(y, z)]
                for s, n in y_steps:
                    spots = [(a + s * k, b) for a, b in spots for k in range(n)]
                for s, n in z_steps:
                    spots = [(a, b + s * k) for a, b in spots for k in range(n)]
                for x in range(xs):
                    groups.append([((a * zs + b) * xs + x) * 2 + core for a, b in spots])
    return groups


def exchanged(pieces, axis, groups=None):
    return lax.all_to_all(pieces, axis, 0, 0, axis_index_groups=groups)


def spread(block, count):
    return jnp.broadcast_to(block[None], (count, *block.shape))


def total(pieces):
    return jnp.sum(pieces.astype(jnp.float32), axis=0)


def body(sizes, hidden, test_matrix):
    bf16 = jnp.bfloat16
    tok_rows, width = hidden.shape
    tile = tok_rows // 8
    ys, zs, xs = sizes
    total_rows = tok_rows * ys * zs
    core = lax.axis_index("core")
    mine, other = core.reshape(1), (1 - core).reshape(1)

    send = streamed_half(hidden, test_matrix, other)
    send, hidden, test_matrix = lax.optimization_barrier((send, hidden, test_matrix))
    landed = swapped(send)
    half_first = (half_product(half_kernel, hidden, test_matrix, mine) + landed).astype(bf16)
    my_half = (total(exchanged(spread(half_first, xs), "x")) * (1.0 / math.sqrt(D))).astype(bf16)
    other_half = swapped(my_half)
    local_back = half_back(hidden, my_half, mine, jnp.float32)
    local_back = half_back(hidden, other_half, other, bf16, local_back)

    pieces = local_back.reshape(ys * zs, K // (ys * zs), width)
    my_back = (total(exchanged(pieces, ROW)) * (1.0 / total_rows)).astype(bf16)
    back = exchanged(spread(my_back, ys * zs), ROW).reshape(K, width)

    landed = swapped(half_product(striped_kernel, hidden, back, other))
    kept = half_product(striped_kernel, hidden, back, mine)
    pieces = exchanged((kept + landed).astype(bf16).reshape(xs, tile, K), "x")
    my_rows, gram = rows_and_gram(lax.axis_index("x").reshape(1), pieces, kept, landed, 1.0 / total_rows)
    gram = total(exchanged(gram.reshape(8, 3 * HALF // 8, HALF), COL))
    lines = [((), ((1, zs),)), (((1, ys),), ())]
    for along in (lines, lines[::-1]):
        groups = line_groups(sizes, along)
        gram = total(exchanged(spread(gram, len(groups[0])), ALL, groups))
    gram = exchanged(spread(gram, 8), COL).reshape(3 * HALF, HALF)
    return factor_call(gram, my_rows)


def solution(mesh):
    rows, cols = mesh.devices.shape
    side = math.isqrt(rows)
    sizes = (side, rows // side, cols // 2)
    grid = Mesh(mesh.devices.reshape(*sizes, 2), ALL)
    in_specs = (P(ROW, COL), P(COL, None))
    out_specs = (P(ALL, None), P())
    return jax.shard_map(
        lambda *args: body(sizes, *args), mesh=grid, in_specs=in_specs, out_specs=out_specs, check_vma=False
    )
```

```python
import math

import jax
import jax.numpy as jnp
from jax import lax
from jax.experimental import pallas as pl
from jax.experimental.pallas import tpu as pltpu
from jax.sharding import Mesh, PartitionSpec as P

D = 7168
K = 256
HALF = K // 2
HIGH = lax.Precision.HIGHEST

def dot(a, b, over_a=1, over_b=0, precision=None):
    return lax.dot_general(
        a, b, (((over_a,), (over_b,)), ((), ())), precision=precision, preferred_element_type=jnp.float32
    )


def terms(a, count):
    parts = []
    for _ in range(count):
        parts.append(a.astype(jnp.bfloat16))
        a = a - parts[-1].astype(jnp.float32)
    return parts


def factor_kernel(packed_ref, rows_ref, basis_ref, factor_ref, gram_ref, g_ref, x_ref, work_ref):
    bf16 = jnp.bfloat16
    corner = packed_ref[HALF : 2 * HALF, :]
    gram_ref[:HALF, :HALF] = packed_ref[:HALF, :]
    gram_ref[:HALF, HALF:] = corner
    gram_ref[HALF:, :HALF] = corner.T
    gram_ref[HALF:, HALF:] = packed_ref[2 * HALF :, :]
    row = lax.broadcasted_iota(jnp.int32, (K, K), 0)
    col = lax.broadcasted_iota(jnp.int32, (K, K), 1)
    eye = (row == col).astype(jnp.float32)
    upper = jnp.where(row < col, 1.0, jnp.where(row == col, 0.5, 0.0))
    on_diag = jnp.where(row == col, gram_ref[...], 0.0)
    s_row = lax.rsqrt(jnp.sum(on_diag, axis=0, keepdims=True))
    s_col = lax.rsqrt(jnp.sum(on_diag, axis=1, keepdims=True))

    def change_for(g):
        f = (g - eye) * upper
        fb = f.astype(bf16)
        a = f - dot(fb, fb, 0, 0) * upper
        ab = a.astype(bf16)
        return (dot(ab, ab) - a).astype(bf16)

    def moved(g, n):
        y = g + sum(dot(part, n) for part in terms(g, 3))
        return y + sum(dot(n, part, 0, 0) for part in terms(y, 3))

    def size(e):
        return jnp.sum(e * e)

    g = gram_ref[...] * s_row * s_col
    n = change_for(g)
    x_ref[...] = s_col * (eye + n.astype(jnp.float32))
    g_ref[...] = moved(g, n)

    def step(state):
        count, _ = state
        g = g_ref[...]
        n = change_for(g)
        g = moved(g, n)
        g_ref[...] = g
        x = x_ref[...]
        x_ref[...] = x + sum(dot(part, n) for part in terms(x, 3))
        return count + 1, size(g - eye)

    def more(state):
        count, err = state
        return jnp.logical_and(count < 12, err > 1e-5)

    _, err = lax.while_loop(more, step, (jnp.int32(0), jnp.float32(1.0)))
    ok = err <= 1e-5

    @pl.when(ok)
    def _():
        x = x_ref[...]
        last = ((g_ref[...] - eye) * upper).astype(bf16)
        x_ref[...] = x - sum(dot(part, last) for part in terms(x, 2))

    @pl.when(jnp.logical_not(ok))
    def _():
        work_ref[:, :K] = gram_ref[...]
        work_ref[:, K:] = eye
        lane = lax.broadcasted_iota(jnp.int32, (1, 2 * K), 1)

        def eliminate(k, carry):
            line = work_ref[pl.ds(k, 1), :]
            pivot = jnp.sum(jnp.where(lane == k, line, 0.0), axis=1, keepdims=True)
            line = line * lax.rsqrt(pivot)
            coef = jnp.where(lane[:, :K] > k, line[:, :K], 0.0)
            work_ref[...] = work_ref[...] - dot(coef, line, 0, 0, HIGH)
            work_ref[pl.ds(k, 1), :] = line
            return carry

        lax.fori_loop(0, K, eliminate, 0)
        x_ref[...] = work_ref[:, K:].T

    x = jnp.where(row <= col, x_ref[...], 0.0)
    basis_ref[...] = dot(rows_ref[...], x, precision=HIGH)
    factor_ref[...] = jnp.where(row <= col, dot(x, gram_ref[...], 0, 0, HIGH), 0.0)


def factor_call(packed, rows):
    square = pltpu.VMEM((K, K), jnp.float32)
    return pl.pallas_call(
        factor_kernel,
        out_shape=(jax.ShapeDtypeStruct(rows.shape, jnp.float32), jax.ShapeDtypeStruct((K, K), jnp.float32)),
        in_specs=[WHOLE] * 2,
        out_specs=(WHOLE, WHOLE),
        scratch_shapes=[square, square, square, pltpu.VMEM((K, 2 * K), jnp.float32)],
        compiler_params=PARAMS,
        name="factor",
    )(packed, rows)


WHOLE = pl.BlockSpec(memory_space=pltpu.VMEM)
PARAMS = pltpu.CompilerParams(vmem_limit_bytes=12 * 1024 * 1024)


def opening_kernel(which_ref, hidden_ref, right_ref, send_ref, hidden_out, sems):
    rows = send_ref.shape[0]
    halves = [pl.ds(pl.multiple_of(half * rows, rows), rows) for half in (which_ref[0], 1 - which_ref[0])]
    copies = [
        pltpu.make_async_copy(hidden_ref.at[half, :], hidden_out.at[half, :], sems.at[i]) for i, half in enumerate(halves)
    ]
    for copy in copies:
        copy.start()
    copies[0].wait()
    send_ref[...] = dot(hidden_out[halves[0], :], right_ref[...])
    copies[1].wait()


def opening(hidden, right, half):
    return pl.pallas_call(
        opening_kernel,
        out_shape=(
            jax.ShapeDtypeStruct((hidden.shape[0] // 2, K), jnp.float32),
            jax.ShapeDtypeStruct(hidden.shape, hidden.dtype),
        ),
        in_specs=[SCALAR, pl.BlockSpec(memory_space=pltpu.HBM), WHOLE],
        out_specs=(WHOLE, WHOLE),
        scratch_shapes=[pltpu.SemaphoreType.DMA((2,))],
        compiler_params=pltpu.CompilerParams(vmem_limit_bytes=49 * 1024 * 1024),
        name="opening",
    )(half, hidden, right)


SCALAR = pl.BlockSpec(memory_space=pltpu.SMEM)


def half_kernel(which_ref, hidden_ref, right_ref, out_ref):
    rows = out_ref.shape[0]
    out_ref[...] = dot(hidden_ref[pl.ds(pl.multiple_of(which_ref[0] * rows, rows), rows), :], right_ref[...])


def striped_kernel(which_ref, hidden_ref, back_ref, out_ref):
    rows = out_ref.shape[0]
    tile = rows // 4
    blocks = [hidden_ref[pl.ds(pl.multiple_of((2 * i + which_ref[0]) * tile, tile), tile), :] for i in range(4)]
    out_ref[...] = dot(jnp.concatenate(blocks, axis=0), back_ref[...], 1, 1)


def half_product(kernel, hidden, right, half):
    return pl.pallas_call(
        kernel,
        out_shape=jax.ShapeDtypeStruct((hidden.shape[0] // 2, K), jnp.float32),
        in_specs=[SCALAR, WHOLE, WHOLE],
        out_specs=WHOLE,
        compiler_params=PARAMS,
        name="half_product",
    )(half, hidden, right)


def back_kernel(which_ref, hidden_ref, first_ref, *refs):
    *so_far, out_ref = refs
    rows = first_ref.shape[0]
    part = dot(first_ref[...], hidden_ref[pl.ds(pl.multiple_of(which_ref[0] * rows, rows), rows), :], 0, 0)
    for ref in so_far:
        part = part + ref[...]
    if len(out_ref.shape) == 2:
        out_ref[...] = part
        return
    count, rows, _ = out_ref.shape
    for i in range(count):
        out_ref[i] = part[i * rows : (i + 1) * rows, :].astype(out_ref.dtype)


def half_back(hidden, first, half, shape, dtype, *so_far):
    return pl.pallas_call(
        back_kernel,
        out_shape=jax.ShapeDtypeStruct(shape, dtype),
        in_specs=[SCALAR, *[WHOLE] * (2 + len(so_far))],
        out_specs=WHOLE,
        compiler_params=PARAMS,
        name="half_back",
    )(half, hidden, first, *so_far)


def join_kernel(pieces_ref, out_ref):
    count, rows, _ = pieces_ref.shape
    step = 16 // rows
    for i in range(0, count, step):
        parts = [pieces_ref[i + j].astype(jnp.float32) for j in range(step)]
        out_ref[i * rows : (i + step) * rows, :] = jnp.concatenate(parts, axis=0).astype(out_ref.dtype)


def joined(pieces):
    count, rows, width = pieces.shape
    return pl.pallas_call(
        join_kernel,
        out_shape=jax.ShapeDtypeStruct((count * rows, width), pieces.dtype),
        in_specs=[WHOLE],
        out_specs=WHOLE,
        compiler_params=PARAMS,
        name="joined",
    )(pieces)


def sum_kernel(x_ref, kept_ref, landed_ref, own_ref, pieces_ref):
    count, tile, _ = pieces_ref.shape
    own = pl.ds(pl.multiple_of(x_ref[0] * tile, tile), tile)
    own_ref[...] = kept_ref[own, :] + landed_ref[own, :]
    for i in range(count):
        block = slice(i * tile, (i + 1) * tile)
        pieces_ref[i] = (kept_ref[block, :] + landed_ref[block, :]).astype(pieces_ref.dtype)


def sum_of_halves(x, kept, landed, count):
    tile = kept.shape[0] // count
    return pl.pallas_call(
        sum_kernel,
        out_shape=(
            jax.ShapeDtypeStruct((tile, K), jnp.float32),
            jax.ShapeDtypeStruct((count, tile, K), jnp.bfloat16),
        ),
        in_specs=[SCALAR, WHOLE, WHOLE],
        out_specs=(WHOLE, WHOLE),
        compiler_params=PARAMS,
        name="sum_of_halves",
    )(x, kept, landed)


def gram_kernel(scale, x_ref, landed_ref, own_ref, rows_ref, packed_ref):
    rows = own_ref[...]
    for i in range(landed_ref.shape[0]):
        rows = rows + jnp.where(x_ref[0] == i, 0.0, landed_ref[i].astype(jnp.float32))
    rows_ref[...] = rows
    left, right = rows[:, :HALF], rows[:, HALF:]
    packed_ref[:HALF, :] = dot(left, left, 0, 0, HIGH) * scale
    packed_ref[HALF : 2 * HALF, :] = dot(left, right, 0, 0, HIGH) * scale
    packed_ref[2 * HALF :, :] = dot(right, right, 0, 0, HIGH) * scale


def rows_and_gram(x, landed, own, scale):
    return pl.pallas_call(
        lambda *refs: gram_kernel(scale, *refs),
        out_shape=(
            jax.ShapeDtypeStruct(landed.shape[1:], jnp.float32),
            jax.ShapeDtypeStruct((3 * HALF, HALF), jnp.float32),
        ),
        in_specs=[SCALAR, WHOLE, WHOLE],
        out_specs=(WHOLE, WHOLE),
        compiler_params=PARAMS,
        name="rows_and_gram",
    )(x, landed, own)


ROW = ("y", "z")
COL = ("x", "core")
ALL = (*ROW, *COL)


def swapped(block):
    return lax.ppermute(block, "core", [(0, 1), (1, 0)])


def line_groups(sizes, along):
    ys, zs, xs = sizes
    groups = []
    for core in range(2):
        y_steps, z_steps = along[core]
        for y in range(ys):
            for z in range(zs):
                if any(y // s % n for s, n in y_steps) or any(z // s % n for s, n in z_steps):
                    continue
                spots = [(y, z)]
                for s, n in y_steps:
                    spots = [(a + s * k, b) for a, b in spots for k in range(n)]
                for s, n in z_steps:
                    spots = [(a, b + s * k) for a, b in spots for k in range(n)]
                for x in range(xs):
                    groups.append([((a * zs + b) * xs + x) * 2 + core for a, b in spots])
    return groups


def exchanged(pieces, axis, groups=None):
    return lax.all_to_all(pieces, axis, 0, 0, axis_index_groups=groups)


def spread(block, count):
    return jnp.broadcast_to(block[None], (count, *block.shape))


def total(pieces):
    return jnp.sum(pieces.astype(jnp.float32), axis=0)


def body(sizes, hidden, test_matrix):
    bf16 = jnp.bfloat16
    tok_rows, width = hidden.shape
    tile = tok_rows // 8
    ys, zs, xs = sizes
    total_rows = tok_rows * ys * zs
    core = lax.axis_index("core")
    mine, other = core.reshape(1), (1 - core).reshape(1)

    send, hidden = opening(hidden, test_matrix, other)
    landed = swapped(send)
    pieces = (half_product(half_kernel, hidden, test_matrix, mine) + landed).astype(bf16).reshape(xs, tile, K)
    my_first = (total(exchanged(pieces, "x")) * (1.0 / math.sqrt(D))).astype(bf16)
    my_half = exchanged(spread(my_first, xs), "x").reshape(tok_rows // 2, K)
    other_half = swapped(my_half)
    local_back = half_back(hidden, my_half, mine, (K, width), jnp.float32)
    shape = (ys * zs, K // (ys * zs), width)
    pieces = half_back(hidden, other_half, other, shape, bf16, local_back)

    my_back = (total(exchanged(pieces, ROW)) * (1.0 / total_rows)).astype(bf16)
    back = joined(exchanged(spread(my_back, ys * zs), ROW))

    landed = swapped(half_product(striped_kernel, hidden, back, other))
    kept = half_product(striped_kernel, hidden, back, mine)
    x = lax.axis_index("x").reshape(1)
    own, pieces = sum_of_halves(x, kept, landed, xs)
    my_rows, gram = rows_and_gram(x, exchanged(pieces, "x"), own, 1.0 / total_rows)
    gram = total(exchanged(gram.reshape(8, 3 * HALF // 8, HALF), COL))
    lines = [((), ((1, zs),)), (((1, ys),), ())]
    for along in (lines, lines[::-1]):
        groups = line_groups(sizes, along)
        gram = total(exchanged(spread(gram, len(groups[0])), ALL, groups))
    gram = exchanged(spread(gram, 8), COL).reshape(3 * HALF, HALF)
    return factor_call(gram, my_rows)


def solution(mesh):
    rows, cols = mesh.devices.shape
    side = math.isqrt(rows)
    sizes = (side, rows // side, cols // 2)
    grid = Mesh(mesh.devices.reshape(*sizes, 2), ALL)
    in_specs = (P(ROW, COL), P(COL, None))
    out_specs = (P(ALL, None), P())
    return jax.shard_map(
        lambda *args: body(sizes, *args), mesh=grid, in_specs=in_specs, out_specs=out_specs, check_vma=False
    )
```

```python
import math

import jax
import jax.numpy as jnp
from jax import lax
from jax.experimental import pallas as pl
from jax.experimental.pallas import tpu as pltpu
from jax.sharding import Mesh, PartitionSpec as P

D = 7168
K = 256
HALF = K // 2
HIGH = lax.Precision.HIGHEST

def dot(a, b, over_a=1, over_b=0, precision=None):
    return lax.dot_general(
        a, b, (((over_a,), (over_b,)), ((), ())), precision=precision, preferred_element_type=jnp.float32
    )


def terms(a, count):
    parts = []
    for _ in range(count):
        parts.append(a.astype(jnp.bfloat16))
        a = a - parts[-1].astype(jnp.float32)
    return parts


def factor_kernel(packed_ref, rows_ref, basis_ref, factor_ref, gram_ref, g_ref, x_ref, work_ref):
    bf16 = jnp.bfloat16
    corner = packed_ref[HALF : 2 * HALF, :]
    gram_ref[:HALF, :HALF] = packed_ref[:HALF, :]
    gram_ref[:HALF, HALF:] = corner
    gram_ref[HALF:, :HALF] = corner.T
    gram_ref[HALF:, HALF:] = packed_ref[2 * HALF :, :]
    row = lax.broadcasted_iota(jnp.int32, (K, K), 0)
    col = lax.broadcasted_iota(jnp.int32, (K, K), 1)
    eye = (row == col).astype(jnp.float32)
    upper = jnp.where(row < col, 1.0, jnp.where(row == col, 0.5, 0.0))
    on_diag = jnp.where(row == col, gram_ref[...], 0.0)
    s_row = lax.rsqrt(jnp.sum(on_diag, axis=0, keepdims=True))
    s_col = lax.rsqrt(jnp.sum(on_diag, axis=1, keepdims=True))

    def change_for(g):
        f = (g - eye) * upper
        fb = f.astype(bf16)
        a = f - dot(fb, fb, 0, 0) * upper
        ab = a.astype(bf16)
        return (dot(ab, ab) - a).astype(bf16)

    def moved(g, n):
        y = g + sum(dot(part, n) for part in terms(g, 3))
        return y + sum(dot(n, part, 0, 0) for part in terms(y, 3))

    def size(e):
        return jnp.sum(e * e)

    g = gram_ref[...] * s_row * s_col
    n = change_for(g)
    x_ref[...] = s_col * (eye + n.astype(jnp.float32))
    g_ref[...] = moved(g, n)

    def step(state):
        count, _ = state
        g = g_ref[...]
        n = change_for(g)
        g = moved(g, n)
        g_ref[...] = g
        x = x_ref[...]
        x_ref[...] = x + sum(dot(part, n) for part in terms(x, 3))
        return count + 1, size(g - eye)

    def more(state):
        count, err = state
        return jnp.logical_and(count < 12, err > 1e-5)

    _, err = lax.while_loop(more, step, (jnp.int32(0), jnp.float32(1.0)))
    ok = err <= 1e-5

    @pl.when(ok)
    def _():
        x = x_ref[...]
        last = ((g_ref[...] - eye) * upper).astype(bf16)
        x_ref[...] = x - sum(dot(part, last) for part in terms(x, 2))

    @pl.when(jnp.logical_not(ok))
    def _():
        work_ref[:, :K] = gram_ref[...]
        work_ref[:, K:] = eye
        lane = lax.broadcasted_iota(jnp.int32, (1, 2 * K), 1)

        def eliminate(k, carry):
            line = work_ref[pl.ds(k, 1), :]
            pivot = jnp.sum(jnp.where(lane == k, line, 0.0), axis=1, keepdims=True)
            line = line * lax.rsqrt(pivot)
            coef = jnp.where(lane[:, :K] > k, line[:, :K], 0.0)
            work_ref[...] = work_ref[...] - dot(coef, line, 0, 0, HIGH)
            work_ref[pl.ds(k, 1), :] = line
            return carry

        lax.fori_loop(0, K, eliminate, 0)
        x_ref[...] = work_ref[:, K:].T

    x = jnp.where(row <= col, x_ref[...], 0.0)
    basis_ref[...] = dot(rows_ref[...], x, precision=HIGH)
    factor_ref[...] = jnp.where(row <= col, dot(x, gram_ref[...], 0, 0, HIGH), 0.0)


def factor_call(packed, rows):
    square = pltpu.VMEM((K, K), jnp.float32)
    return pl.pallas_call(
        factor_kernel,
        out_shape=(jax.ShapeDtypeStruct(rows.shape, jnp.float32), jax.ShapeDtypeStruct((K, K), jnp.float32)),
        in_specs=[WHOLE] * 2,
        out_specs=(WHOLE, WHOLE),
        scratch_shapes=[square, square, square, pltpu.VMEM((K, 2 * K), jnp.float32)],
        compiler_params=PARAMS,
        name="factor",
    )(packed, rows)


WHOLE = pl.BlockSpec(memory_space=pltpu.VMEM)
PARAMS = pltpu.CompilerParams(vmem_limit_bytes=12 * 1024 * 1024)


def opening_kernel(which_ref, hidden_ref, right_ref, send_ref, hidden_out, sems):
    rows = send_ref.shape[0]
    halves = [pl.ds(pl.multiple_of(half * rows, rows), rows) for half in (which_ref[0], 1 - which_ref[0])]
    copies = [
        pltpu.make_async_copy(hidden_ref.at[half, :], hidden_out.at[half, :], sems.at[i]) for i, half in enumerate(halves)
    ]
    for copy in copies:
        copy.start()
    copies[0].wait()
    send_ref[...] = dot(hidden_out[halves[0], :], right_ref[...])
    copies[1].wait()


def opening(hidden, right, half):
    return pl.pallas_call(
        opening_kernel,
        out_shape=(
            jax.ShapeDtypeStruct((hidden.shape[0] // 2, K), jnp.float32),
            jax.ShapeDtypeStruct(hidden.shape, hidden.dtype),
        ),
        in_specs=[SCALAR, pl.BlockSpec(memory_space=pltpu.HBM), WHOLE],
        out_specs=(WHOLE, WHOLE),
        scratch_shapes=[pltpu.SemaphoreType.DMA((2,))],
        compiler_params=pltpu.CompilerParams(vmem_limit_bytes=49 * 1024 * 1024),
        name="opening",
    )(half, hidden, right)


SCALAR = pl.BlockSpec(memory_space=pltpu.SMEM)


def half_kernel(which_ref, hidden_ref, right_ref, out_ref):
    rows = out_ref.shape[0]
    out_ref[...] = dot(hidden_ref[pl.ds(pl.multiple_of(which_ref[0] * rows, rows), rows), :], right_ref[...])


def striped_kernel(which_ref, hidden_ref, back_ref, out_ref):
    rows = out_ref.shape[0]
    tile = rows // 4
    blocks = [hidden_ref[pl.ds(pl.multiple_of((2 * i + which_ref[0]) * tile, tile), tile), :] for i in range(4)]
    out_ref[...] = dot(jnp.concatenate(blocks, axis=0), back_ref[...], 1, 1)


def half_product(kernel, hidden, right, half):
    return pl.pallas_call(
        kernel,
        out_shape=jax.ShapeDtypeStruct((hidden.shape[0] // 2, K), jnp.float32),
        in_specs=[SCALAR, WHOLE, WHOLE],
        out_specs=WHOLE,
        compiler_params=PARAMS,
        name="half_product",
    )(half, hidden, right)


def back_kernel(which_ref, hidden_ref, first_ref, *refs):
    *so_far, out_ref = refs
    rows = first_ref.shape[0]
    part = dot(first_ref[...], hidden_ref[pl.ds(pl.multiple_of(which_ref[0] * rows, rows), rows), :], 0, 0)
    for ref in so_far:
        part = part + ref[...]
    out_ref[...] = part.astype(out_ref.dtype)


def half_back(hidden, first, half, dtype, *so_far):
    return pl.pallas_call(
        back_kernel,
        out_shape=jax.ShapeDtypeStruct((K, hidden.shape[1]), dtype),
        in_specs=[SCALAR, *[WHOLE] * (2 + len(so_far))],
        out_specs=WHOLE,
        compiler_params=PARAMS,
        name="half_back",
    )(half, hidden, first, *so_far)


def gram_kernel(scale, landed_ref, rows_ref, packed_ref):
    rows = landed_ref[0]
    for i in range(1, landed_ref.shape[0]):
        rows = rows + landed_ref[i]
    rows_ref[...] = rows
    left, right = rows[:, :HALF], rows[:, HALF:]
    packed_ref[:HALF, :] = dot(left, left, 0, 0, HIGH) * scale
    packed_ref[HALF : 2 * HALF, :] = dot(left, right, 0, 0, HIGH) * scale
    packed_ref[2 * HALF :, :] = dot(right, right, 0, 0, HIGH) * scale


def rows_and_gram(landed, scale):
    return pl.pallas_call(
        lambda *refs: gram_kernel(scale, *refs),
        out_shape=(
            jax.ShapeDtypeStruct(landed.shape[1:], jnp.float32),
            jax.ShapeDtypeStruct((3 * HALF, HALF), jnp.float32),
        ),
        in_specs=[WHOLE],
        out_specs=(WHOLE, WHOLE),
        compiler_params=PARAMS,
        name="rows_and_gram",
    )(landed)


ROW = ("y", "z")
COL = ("x", "core")
ALL = (*ROW, *COL)


def swapped(block):
    return lax.ppermute(block, "core", [(0, 1), (1, 0)])


def line_groups(sizes, along):
    ys, zs, xs = sizes
    groups = []
    for core in range(2):
        y_steps, z_steps = along[core]
        for y in range(ys):
            for z in range(zs):
                if any(y // s % n for s, n in y_steps) or any(z // s % n for s, n in z_steps):
                    continue
                spots = [(y, z)]
                for s, n in y_steps:
                    spots = [(a + s * k, b) for a, b in spots for k in range(n)]
                for s, n in z_steps:
                    spots = [(a, b + s * k) for a, b in spots for k in range(n)]
                for x in range(xs):
                    groups.append([((a * zs + b) * xs + x) * 2 + core for a, b in spots])
    return groups


def exchanged(pieces, axis, groups=None):
    return lax.all_to_all(pieces, axis, 0, 0, axis_index_groups=groups)


def spread(block, count):
    return jnp.broadcast_to(block[None], (count, *block.shape))


def total(pieces):
    return jnp.sum(pieces.astype(jnp.float32), axis=0)


def body(sizes, hidden, test_matrix):
    bf16 = jnp.bfloat16
    tok_rows, width = hidden.shape
    tile = tok_rows // 8
    ys, zs, xs = sizes
    total_rows = tok_rows * ys * zs
    core = lax.axis_index("core")
    mine, other = core.reshape(1), (1 - core).reshape(1)

    send, hidden = opening(hidden, test_matrix, other)
    landed = swapped(send)
    pieces = (half_product(half_kernel, hidden, test_matrix, mine) + landed).astype(bf16).reshape(xs, tile, K)
    my_first = (total(exchanged(pieces, "x")) * (1.0 / math.sqrt(D))).astype(bf16)
    my_half = exchanged(spread(my_first, xs), "x").reshape(tok_rows // 2, K)
    other_half = swapped(my_half)
    local_back = half_back(hidden, my_half, mine, jnp.float32)
    local_back = half_back(hidden, other_half, other, bf16, local_back)

    lines = ((), ((1, zs),)), (((1, ys),), ())
    this_way, that_way = line_groups(sizes, lines), line_groups(sizes, lines[::-1])
    count = len(this_way[0])
    pieces = local_back.reshape(count, K // count, width)
    my_back = total(exchanged(pieces, ALL, this_way)).astype(bf16)
    my_back = total(exchanged(spread(my_back, len(that_way[0])), ALL, that_way))
    my_back = (my_back * (1.0 / total_rows)).astype(bf16)
    back = exchanged(spread(my_back, count), ALL, this_way).reshape(K, width)

    landed = swapped(half_product(striped_kernel, hidden, back, other))
    pieces = (half_product(striped_kernel, hidden, back, mine) + landed).reshape(xs, tile, K)
    my_rows, gram = rows_and_gram(exchanged(pieces, "x"), 1.0 / total_rows)
    gram = total(exchanged(gram.reshape(8, 3 * HALF // 8, HALF), COL))
    for groups in (this_way, that_way):
        gram = total(exchanged(spread(gram, len(groups[0])), ALL, groups))
    gram = exchanged(spread(gram, 8), COL).reshape(3 * HALF, HALF)
    return factor_call(gram, my_rows)


def solution(mesh):
    rows, cols = mesh.devices.shape
    side = math.isqrt(rows)
    sizes = (side, rows // side, cols // 2)
    grid = Mesh(mesh.devices.reshape(*sizes, 2), ALL)
    in_specs = (P(ROW, COL), P(COL, None))
    out_specs = (P(ALL, None), P())
    return jax.shard_map(
        lambda *args: body(sizes, *args), mesh=grid, in_specs=in_specs, out_specs=out_specs, check_vma=False
    )
```

```python
import math

import jax
import jax.numpy as jnp
from jax import lax
from jax.experimental import pallas as pl
from jax.experimental.pallas import tpu as pltpu
from jax.sharding import Mesh, PartitionSpec as P

D = 7168
K = 256
HALF = K // 2
HIGH = lax.Precision.HIGHEST

def dot(a, b, over_a=1, over_b=0, precision=None):
    return lax.dot_general(
        a, b, (((over_a,), (over_b,)), ((), ())), precision=precision, preferred_element_type=jnp.float32
    )


def terms(a):
    high = a.astype(jnp.bfloat16)
    return high, (a - high.astype(jnp.float32)).astype(jnp.bfloat16)


def factor_kernel(packed_ref, rows_ref, basis_ref, factor_ref, gram_ref, g_ref, x_ref, work_ref):
    bf16 = jnp.bfloat16
    corner = packed_ref[HALF : 2 * HALF, :]
    gram_ref[:HALF, :HALF] = packed_ref[:HALF, :]
    gram_ref[:HALF, HALF:] = corner
    gram_ref[HALF:, :HALF] = corner.T
    gram_ref[HALF:, HALF:] = packed_ref[2 * HALF :, :]
    row = lax.broadcasted_iota(jnp.int32, (K, K), 0)
    col = lax.broadcasted_iota(jnp.int32, (K, K), 1)
    eye = (row == col).astype(jnp.float32)
    upper = jnp.where(row < col, 1.0, jnp.where(row == col, 0.5, 0.0))
    on_diag = jnp.where(row == col, gram_ref[...], 0.0)
    s_row = lax.rsqrt(jnp.sum(on_diag, axis=0, keepdims=True))
    s_col = lax.rsqrt(jnp.sum(on_diag, axis=1, keepdims=True))

    def change_for(g):
        f = (g - eye) * upper
        fb = f.astype(bf16)
        a = f - dot(fb, fb, 0, 0) * upper
        ab = a.astype(bf16)
        return (dot(ab, ab) - a).astype(bf16)

    def moved(g, n):
        y = g + sum(dot(part, n) for part in terms(g))
        return y + sum(dot(n, part, 0, 0) for part in terms(y))

    def size(e):
        return jnp.sum(e * e)

    g = gram_ref[...] * s_row * s_col
    n = change_for(g)
    x_ref[...] = s_col * (eye + n.astype(jnp.float32))
    g_ref[...] = moved(g, n)

    def step(state):
        count, _ = state
        g = g_ref[...]
        n = change_for(g)
        g = moved(g, n)
        g_ref[...] = g
        x = x_ref[...]
        x_ref[...] = x + sum(dot(part, n) for part in terms(x))
        return count + 1, size(g - eye)

    def more(state):
        count, err = state
        return jnp.logical_and(count < 12, err > 1e-5)

    _, err = lax.while_loop(more, step, (jnp.int32(0), jnp.float32(1.0)))
    ok = err <= 1e-5

    @pl.when(ok)
    def _():
        x = x_ref[...]
        last = ((g_ref[...] - eye) * upper).astype(bf16)
        x_ref[...] = x - dot(x.astype(bf16), last)

    @pl.when(jnp.logical_not(ok))
    def _():
        work_ref[:, :K] = gram_ref[...]
        work_ref[:, K:] = eye
        lane = lax.broadcasted_iota(jnp.int32, (1, 2 * K), 1)

        def eliminate(k, carry):
            line = work_ref[pl.ds(k, 1), :]
            pivot = jnp.sum(jnp.where(lane == k, line, 0.0), axis=1, keepdims=True)
            line = line * lax.rsqrt(pivot)
            coef = jnp.where(lane[:, :K] > k, line[:, :K], 0.0)
            work_ref[...] = work_ref[...] - dot(coef, line, 0, 0, HIGH)
            work_ref[pl.ds(k, 1), :] = line
            return carry

        lax.fori_loop(0, K, eliminate, 0)
        x_ref[...] = work_ref[:, K:].T

    x = jnp.where(row <= col, x_ref[...], 0.0)
    basis_ref[...] = dot(rows_ref[...], x, precision=HIGH)
    factor_ref[...] = jnp.where(row <= col, dot(x, gram_ref[...], 0, 0, HIGH), 0.0)


def factor_call(packed, rows):
    square = pltpu.VMEM((K, K), jnp.float32)
    return pl.pallas_call(
        factor_kernel,
        out_shape=(jax.ShapeDtypeStruct(rows.shape, jnp.float32), jax.ShapeDtypeStruct((K, K), jnp.float32)),
        in_specs=[WHOLE] * 2,
        out_specs=(WHOLE, WHOLE),
        scratch_shapes=[square, square, square, pltpu.VMEM((K, 2 * K), jnp.float32)],
        compiler_params=PARAMS,
        name="factor",
    )(packed, rows)


WHOLE = pl.BlockSpec(memory_space=pltpu.VMEM)
PARAMS = pltpu.CompilerParams(vmem_limit_bytes=12 * 1024 * 1024)


def opening_kernel(which_ref, hidden_ref, right_ref, send_ref, hidden_out, sems):
    rows = send_ref.shape[0]
    halves = [pl.ds(pl.multiple_of(half * rows, rows), rows) for half in (which_ref[0], 1 - which_ref[0])]
    copies = [
        pltpu.make_async_copy(hidden_ref.at[half, :], hidden_out.at[half, :], sems.at[i]) for i, half in enumerate(halves)
    ]
    for copy in copies:
        copy.start()
    copies[0].wait()
    send_ref[...] = dot(hidden_out[halves[0], :], right_ref[...]).astype(send_ref.dtype)
    copies[1].wait()


def opening(hidden, right, half):
    return pl.pallas_call(
        opening_kernel,
        out_shape=(
            jax.ShapeDtypeStruct((hidden.shape[0] // 2, K), jnp.bfloat16),
            jax.ShapeDtypeStruct(hidden.shape, hidden.dtype),
        ),
        in_specs=[SCALAR, pl.BlockSpec(memory_space=pltpu.HBM), WHOLE],
        out_specs=(WHOLE, WHOLE),
        scratch_shapes=[pltpu.SemaphoreType.DMA((2,))],
        compiler_params=pltpu.CompilerParams(vmem_limit_bytes=49 * 1024 * 1024),
        name="opening",
    )(half, hidden, right)


SCALAR = pl.BlockSpec(memory_space=pltpu.SMEM)


def half_kernel(which_ref, hidden_ref, right_ref, out_ref):
    rows = out_ref.shape[0]
    out_ref[...] = dot(hidden_ref[pl.ds(pl.multiple_of(which_ref[0] * rows, rows), rows), :], right_ref[...])


def striped_kernel(which_ref, hidden_ref, back_ref, out_ref):
    rows = out_ref.shape[0]
    tile = rows // 4
    blocks = [hidden_ref[pl.ds(pl.multiple_of((2 * i + which_ref[0]) * tile, tile), tile), :] for i in range(4)]
    out_ref[...] = dot(jnp.concatenate(blocks, axis=0), back_ref[...], 1, 1)


def half_product(kernel, hidden, right, half):
    return pl.pallas_call(
        kernel,
        out_shape=jax.ShapeDtypeStruct((hidden.shape[0] // 2, K), jnp.float32),
        in_specs=[SCALAR, WHOLE, WHOLE],
        out_specs=WHOLE,
        compiler_params=PARAMS,
        name="half_product",
    )(half, hidden, right)


def back_kernel(which_ref, hidden_ref, first_ref, *refs):
    *so_far, out_ref = refs
    rows = first_ref.shape[0]
    part = dot(first_ref[...], hidden_ref[pl.ds(pl.multiple_of(which_ref[0] * rows, rows), rows), :], 0, 0)
    for ref in so_far:
        part = part + ref[...]
    out_ref[...] = part.astype(out_ref.dtype)


def half_back(hidden, first, half, dtype, *so_far):
    return pl.pallas_call(
        back_kernel,
        out_shape=jax.ShapeDtypeStruct((K, hidden.shape[1]), dtype),
        in_specs=[SCALAR, *[WHOLE] * (2 + len(so_far))],
        out_specs=WHOLE,
        compiler_params=PARAMS,
        name="half_back",
    )(half, hidden, first, *so_far)


def split_kernel(x_ref, whole_ref, own_ref, pieces_ref):
    count, tile, _ = pieces_ref.shape
    own_ref[...] = whole_ref[pl.ds(pl.multiple_of(x_ref[0] * tile, tile), tile), :]
    for i in range(count):
        pieces_ref[i] = whole_ref[i * tile : (i + 1) * tile, :].astype(pieces_ref.dtype)


def own_and_pieces(x, whole, count):
    tile = whole.shape[0] // count
    return pl.pallas_call(
        split_kernel,
        out_shape=(
            jax.ShapeDtypeStruct((tile, K), jnp.float32),
            jax.ShapeDtypeStruct((count, tile, K), jnp.bfloat16),
        ),
        in_specs=[SCALAR, WHOLE],
        out_specs=(WHOLE, WHOLE),
        compiler_params=PARAMS,
        name="own_and_pieces",
    )(x, whole)


def gram_kernel(scale, x_ref, landed_ref, own_ref, rows_ref, packed_ref):
    rows = own_ref[...]
    for i in range(landed_ref.shape[0]):
        rows = rows + jnp.where(x_ref[0] == i, 0.0, landed_ref[i].astype(jnp.float32))
    rows_ref[...] = rows
    left, right = rows[:, :HALF], rows[:, HALF:]
    packed_ref[:HALF, :] = dot(left, left, 0, 0, HIGH) * scale
    packed_ref[HALF : 2 * HALF, :] = dot(left, right, 0, 0, HIGH) * scale
    packed_ref[2 * HALF :, :] = dot(right, right, 0, 0, HIGH) * scale


def rows_and_gram(x, landed, own, scale):
    return pl.pallas_call(
        lambda *refs: gram_kernel(scale, *refs),
        out_shape=(
            jax.ShapeDtypeStruct(landed.shape[1:], jnp.float32),
            jax.ShapeDtypeStruct((3 * HALF, HALF), jnp.float32),
        ),
        in_specs=[SCALAR, WHOLE, WHOLE],
        out_specs=(WHOLE, WHOLE),
        compiler_params=PARAMS,
        name="rows_and_gram",
    )(x, landed, own)


ROW = ("y", "z")
COL = ("x", "core")
ALL = (*ROW, *COL)


def swapped(block):
    return lax.ppermute(block, "core", [(0, 1), (1, 0)])


def line_groups(sizes, along):
    ys, zs, xs = sizes
    groups = []
    for core in range(2):
        y_steps, z_steps = along[core]
        for y in range(ys):
            for z in range(zs):
                if any(y // s % n for s, n in y_steps) or any(z // s % n for s, n in z_steps):
                    continue
                spots = [(y, z)]
                for s, n in y_steps:
                    spots = [(a + s * k, b) for a, b in spots for k in range(n)]
                for s, n in z_steps:
                    spots = [(a, b + s * k) for a, b in spots for k in range(n)]
                for x in range(xs):
                    groups.append([((a * zs + b) * xs + x) * 2 + core for a, b in spots])
    return groups


def exchanged(pieces, axis, groups=None):
    return lax.all_to_all(pieces, axis, 0, 0, axis_index_groups=groups)


def spread(block, count):
    return jnp.broadcast_to(block[None], (count, *block.shape))


def total(pieces):
    return jnp.sum(pieces.astype(jnp.float32), axis=0)


def body(sizes, hidden, test_matrix):
    bf16 = jnp.bfloat16
    tok_rows, width = hidden.shape
    tile = tok_rows // 8
    ys, zs, xs = sizes
    total_rows = tok_rows * ys * zs
    core = lax.axis_index("core")
    mine, other = core.reshape(1), (1 - core).reshape(1)

    send, hidden = opening(hidden, test_matrix, other)
    landed = swapped(send)
    pieces = (half_product(half_kernel, hidden, test_matrix, mine) + landed).astype(bf16).reshape(xs, tile, K)
    my_first = (total(exchanged(pieces, "x")) * (1.0 / math.sqrt(D))).astype(bf16)
    my_half = exchanged(spread(my_first, xs), "x").reshape(tok_rows // 2, K)
    other_half = swapped(my_half)
    local_back = half_back(hidden, my_half, mine, jnp.float32)
    local_back = half_back(hidden, other_half, other, bf16, local_back)

    lines = ((), ((1, zs),)), (((1, ys),), ())
    this_way, that_way = line_groups(sizes, lines), line_groups(sizes, lines[::-1])
    count = len(this_way[0])
    pieces = local_back.reshape(count, K // count, width)
    my_back = total(exchanged(pieces, ALL, this_way)).astype(bf16)
    my_back = total(exchanged(spread(my_back, len(that_way[0])), ALL, that_way))
    my_back = (my_back * (1.0 / total_rows)).astype(bf16)
    back = exchanged(spread(my_back, count), ALL, this_way).reshape(K, width)

    landed = swapped(half_product(striped_kernel, hidden, back, other))
    whole = half_product(striped_kernel, hidden, back, mine) + landed
    x = lax.axis_index("x").reshape(1)
    own, pieces = own_and_pieces(x, whole, xs)
    my_rows, gram = rows_and_gram(x, exchanged(pieces, "x"), own, 1.0 / total_rows)
    gram = total(exchanged(gram.reshape(8, 3 * HALF // 8, HALF), COL))
    for groups in (this_way, that_way):
        gram = total(exchanged(spread(gram, len(groups[0])), ALL, groups))
    gram = exchanged(spread(gram, 8), COL).reshape(3 * HALF, HALF)
    return factor_call(gram, my_rows)


def solution(mesh):
    rows, cols = mesh.devices.shape
    side = math.isqrt(rows)
    sizes = (side, rows // side, cols // 2)
    grid = Mesh(mesh.devices.reshape(*sizes, 2), ALL)
    in_specs = (P(ROW, COL), P(COL, None))
    out_specs = (P(ALL, None), P())
    return jax.shard_map(
        lambda *args: body(sizes, *args), mesh=grid, in_specs=in_specs, out_specs=out_specs, check_vma=False
    )
```

```python
import math

import jax
import jax.numpy as jnp
from jax import lax
from jax.experimental import pallas as pl
from jax.experimental.pallas import tpu as pltpu
from jax.sharding import Mesh, PartitionSpec as P

D = 7168
K = 256
HALF = K // 2
HIGH = lax.Precision.HIGHEST

def dot(a, b, over_a=1, over_b=0, precision=None):
    return lax.dot_general(
        a, b, (((over_a,), (over_b,)), ((), ())), precision=precision, preferred_element_type=jnp.float32
    )


def terms(a):
    high = a.astype(jnp.bfloat16)
    return high, (a - high.astype(jnp.float32)).astype(jnp.bfloat16)


def factor_kernel(packed_ref, rows_ref, basis_ref, factor_ref, gram_ref, g_ref, x_ref, work_ref):
    bf16 = jnp.bfloat16
    corner = packed_ref[HALF : 2 * HALF, :]
    gram_ref[:HALF, :HALF] = packed_ref[:HALF, :]
    gram_ref[:HALF, HALF:] = corner
    gram_ref[HALF:, :HALF] = corner.T
    gram_ref[HALF:, HALF:] = packed_ref[2 * HALF :, :]
    row = lax.broadcasted_iota(jnp.int32, (K, K), 0)
    col = lax.broadcasted_iota(jnp.int32, (K, K), 1)
    eye = (row == col).astype(jnp.float32)
    upper = jnp.where(row < col, 1.0, jnp.where(row == col, 0.5, 0.0))
    on_diag = jnp.where(row == col, gram_ref[...], 0.0)
    s_row = lax.rsqrt(jnp.sum(on_diag, axis=0, keepdims=True))
    s_col = lax.rsqrt(jnp.sum(on_diag, axis=1, keepdims=True))

    def change_for(g):
        f = (g - eye) * upper
        fb = f.astype(bf16)
        a = f - dot(fb, fb, 0, 0) * upper
        ab = a.astype(bf16)
        return (dot(ab, ab) - a).astype(bf16)

    def moved(g, n):
        y = g + sum(dot(part, n) for part in terms(g))
        return y + sum(dot(n, part, 0, 0) for part in terms(y))

    def size(e):
        return jnp.sum(e * e)

    g = gram_ref[...] * s_row * s_col
    n = change_for(g)
    x_ref[...] = s_col * (eye + n.astype(jnp.float32))
    g_ref[...] = moved(g, n)

    def step(state):
        count, _ = state
        g = g_ref[...]
        n = change_for(g)
        g = moved(g, n)
        g_ref[...] = g
        x = x_ref[...]
        x_ref[...] = x + sum(dot(part, n) for part in terms(x))
        return count + 1, size(g - eye)

    def more(state):
        count, err = state
        return jnp.logical_and(count < 12, err > 1e-5)

    _, err = lax.while_loop(more, step, (jnp.int32(0), jnp.float32(1.0)))
    ok = err <= 1e-5

    @pl.when(ok)
    def _():
        x = x_ref[...]
        last = ((g_ref[...] - eye) * upper).astype(bf16)
        x_ref[...] = x - dot(x.astype(bf16), last)

    @pl.when(jnp.logical_not(ok))
    def _():
        work_ref[:, :K] = gram_ref[...]
        work_ref[:, K:] = eye
        lane = lax.broadcasted_iota(jnp.int32, (1, 2 * K), 1)

        def eliminate(k, carry):
            line = work_ref[pl.ds(k, 1), :]
            pivot = jnp.sum(jnp.where(lane == k, line, 0.0), axis=1, keepdims=True)
            line = line * lax.rsqrt(pivot)
            coef = jnp.where(lane[:, :K] > k, line[:, :K], 0.0)
            work_ref[...] = work_ref[...] - dot(coef, line, 0, 0, HIGH)
            work_ref[pl.ds(k, 1), :] = line
            return carry

        lax.fori_loop(0, K, eliminate, 0)
        x_ref[...] = work_ref[:, K:].T

    x = jnp.where(row <= col, x_ref[...], 0.0)
    basis_ref[...] = dot(rows_ref[...], x, precision=HIGH)
    factor_ref[...] = jnp.where(row <= col, dot(x, gram_ref[...], 0, 0, HIGH), 0.0)


def factor_call(packed, rows):
    square = pltpu.VMEM((K, K), jnp.float32)
    return pl.pallas_call(
        factor_kernel,
        out_shape=(jax.ShapeDtypeStruct(rows.shape, jnp.float32), jax.ShapeDtypeStruct((K, K), jnp.float32)),
        in_specs=[WHOLE] * 2,
        out_specs=(WHOLE, WHOLE),
        scratch_shapes=[square, square, square, pltpu.VMEM((K, 2 * K), jnp.float32)],
        compiler_params=PARAMS,
        name="factor",
    )(packed, rows)


WHOLE = pl.BlockSpec(memory_space=pltpu.VMEM)
PARAMS = pltpu.CompilerParams(vmem_limit_bytes=12 * 1024 * 1024)


def opening_kernel(place_ref, hidden_ref, right_ref, send_ref, hidden_out, right_out, sems):
    rows = send_ref.shape[0]
    halves = [pl.ds(pl.multiple_of(half * rows, rows), rows) for half in (place_ref[OTHER], place_ref[MINE])]
    copies = [
        pltpu.make_async_copy(right_ref, right_out, sems.at[0]),
        pltpu.make_async_copy(hidden_ref.at[halves[0], :], hidden_out.at[halves[0], :], sems.at[1]),
        pltpu.make_async_copy(hidden_ref.at[halves[1], :], hidden_out.at[halves[1], :], sems.at[2]),
    ]
    for copy in copies:
        copy.start()
    copies[0].wait()
    copies[1].wait()
    send_ref[...] = dot(hidden_out[halves[0], :], right_out[...]).astype(send_ref.dtype)
    copies[2].wait()


def opening(place, hidden, right):
    return pl.pallas_call(
        opening_kernel,
        out_shape=(
            pltpu.VMEM((hidden.shape[0] // 2, K), jnp.bfloat16),
            pltpu.VMEM(hidden.shape, hidden.dtype),
            pltpu.VMEM(right.shape, right.dtype),
        ),
        in_specs=[SCALAR, *[pl.BlockSpec(memory_space=pltpu.HBM)] * 2],
        out_specs=(WHOLE, WHOLE, WHOLE),
        scratch_shapes=[pltpu.SemaphoreType.DMA((3,))],
        compiler_params=pltpu.CompilerParams(vmem_limit_bytes=12 * 1024 * 1024),
        name="opening",
    )(place, pltpu.with_memory_space_constraint(hidden, pltpu.HBM), pltpu.with_memory_space_constraint(right, pltpu.HBM))


SCALAR = pl.BlockSpec(memory_space=pltpu.SMEM)
OTHER, MINE, X = range(3)


def half_kernel(half, place_ref, hidden_ref, right_ref, out_ref):
    rows = out_ref.shape[0]
    out_ref[...] = dot(hidden_ref[pl.ds(pl.multiple_of(place_ref[half] * rows, rows), rows), :], right_ref[...])


def striped_kernel(half, place_ref, hidden_ref, back_ref, out_ref):
    rows = out_ref.shape[0]
    tile = rows // 4
    blocks = [hidden_ref[pl.ds(pl.multiple_of((2 * i + place_ref[half]) * tile, tile), tile), :] for i in range(4)]
    out_ref[...] = dot(jnp.concatenate(blocks, axis=0), back_ref[...], 1, 1)


def half_product(kernel, half, place, hidden, right):
    return pl.pallas_call(
        lambda *refs: kernel(half, *refs),
        out_shape=pltpu.VMEM((hidden.shape[0] // 2, K), jnp.float32),
        in_specs=[SCALAR, WHOLE, WHOLE],
        out_specs=WHOLE,
        compiler_params=PARAMS,
        name="half_product",
    )(place, hidden, right)


def back_kernel(half, place_ref, hidden_ref, first_ref, *refs):
    *so_far, out_ref = refs
    rows = first_ref.shape[0]
    part = dot(first_ref[...], hidden_ref[pl.ds(pl.multiple_of(place_ref[half] * rows, rows), rows), :], 0, 0)
    for ref in so_far:
        part = part + ref[...]
    out_ref[...] = part.astype(out_ref.dtype)


def half_back(half, place, hidden, first, dtype, *so_far):
    return pl.pallas_call(
        lambda *refs: back_kernel(half, *refs),
        out_shape=jax.ShapeDtypeStruct((K, hidden.shape[1]), dtype),
        in_specs=[SCALAR, *[WHOLE] * (2 + len(so_far))],
        out_specs=WHOLE,
        compiler_params=PARAMS,
        name="half_back",
    )(place, hidden, first, *so_far)


def sum_kernel(place_ref, kept_ref, landed_ref, own_ref, pieces_ref):
    count, tile, _ = pieces_ref.shape
    own = pl.ds(pl.multiple_of(place_ref[X] * tile, tile), tile)
    own_ref[...] = kept_ref[own, :] + landed_ref[own, :]
    for i in range(count):
        block = slice(i * tile, (i + 1) * tile)
        pieces_ref[i] = (kept_ref[block, :] + landed_ref[block, :]).astype(pieces_ref.dtype)


def sum_of_halves(place, kept, landed, count):
    tile = kept.shape[0] // count
    return pl.pallas_call(
        sum_kernel,
        out_shape=(
            jax.ShapeDtypeStruct((tile, K), jnp.float32),
            jax.ShapeDtypeStruct((count, tile, K), jnp.bfloat16),
        ),
        in_specs=[SCALAR, WHOLE, WHOLE],
        out_specs=(WHOLE, WHOLE),
        compiler_params=PARAMS,
        name="sum_of_halves",
    )(place, kept, pltpu.with_memory_space_constraint(landed, pltpu.VMEM))


def gram_kernel(scale, place_ref, landed_ref, own_ref, rows_ref, packed_ref):
    rows = own_ref[...]
    for i in range(landed_ref.shape[0]):
        rows = rows + jnp.where(place_ref[X] == i, 0.0, landed_ref[i].astype(jnp.float32))
    rows_ref[...] = rows
    left, right = rows[:, :HALF], rows[:, HALF:]
    packed_ref[:HALF, :] = dot(left, left, 0, 0, HIGH) * scale
    packed_ref[HALF : 2 * HALF, :] = dot(left, right, 0, 0, HIGH) * scale
    packed_ref[2 * HALF :, :] = dot(right, right, 0, 0, HIGH) * scale


def rows_and_gram(place, landed, own, scale):
    return pl.pallas_call(
        lambda *refs: gram_kernel(scale, *refs),
        out_shape=(
            jax.ShapeDtypeStruct(landed.shape[1:], jnp.float32),
            jax.ShapeDtypeStruct((3 * HALF, HALF), jnp.float32),
        ),
        in_specs=[SCALAR, WHOLE, WHOLE],
        out_specs=(WHOLE, WHOLE),
        compiler_params=PARAMS,
        name="rows_and_gram",
    )(place, landed, own)


ROW = ("y_hi", "y_lo", "z")
COL = ("x", "core")
NEAR = ("y_lo", *COL)
ALL = (*ROW, *COL)


def swapped(block):
    return lax.ppermute(block, "core", [(0, 1), (1, 0)])


def line_groups(sizes, along):
    ys, zs, xs = sizes
    groups = []
    for core in range(2):
        y_steps, z_steps = along[core]
        for y in range(ys):
            for z in range(zs):
                if any(y // s % n for s, n in y_steps) or any(z // s % n for s, n in z_steps):
                    continue
                spots = [(y, z)]
                for s, n in y_steps:
                    spots = [(a + s * k, b) for a, b in spots for k in range(n)]
                for s, n in z_steps:
                    spots = [(a, b + s * k) for a, b in spots for k in range(n)]
                for x in range(xs):
                    groups.append([((a * zs + b) * xs + x) * 2 + core for a, b in spots])
    return groups


def exchanged(pieces, axis, groups=None):
    return lax.all_to_all(pieces, axis, 0, 0, axis_index_groups=groups)


def spread(block, count):
    return jnp.broadcast_to(block[None], (count, *block.shape))


def total(pieces):
    return jnp.sum(pieces.astype(jnp.float32), axis=0)


def body(sizes, hidden, test_matrix):
    bf16 = jnp.bfloat16
    tok_rows, width = hidden.shape
    tile = tok_rows // 8
    ys, zs, xs = sizes
    total_rows = tok_rows * ys * zs
    core = lax.axis_index("core")
    place = jnp.stack([1 - core, core, lax.axis_index("x")])

    send, hidden, test_matrix = opening(place, hidden, test_matrix)
    landed = swapped(send)
    pieces = (half_product(half_kernel, MINE, place, hidden, test_matrix) + landed).astype(bf16).reshape(xs, tile, K)
    my_first = (total(exchanged(pieces, "x")) * (1.0 / math.sqrt(D))).astype(bf16)
    my_half = exchanged(spread(my_first, xs), "x").reshape(tok_rows // 2, K)
    other_half = swapped(my_half)
    local_back = half_back(MINE, place, hidden, my_half, jnp.float32)
    local_back = half_back(OTHER, place, hidden, other_half, bf16, local_back)

    lines = ((), ((1, zs),)), (((1, ys),), ())
    this_way, that_way = line_groups(sizes, lines), line_groups(sizes, lines[::-1])
    count = len(this_way[0])
    pieces = local_back.reshape(count, K // count, width)
    my_back = total(exchanged(pieces, ALL, this_way)).astype(bf16)
    my_back = total(exchanged(spread(my_back, len(that_way[0])), ALL, that_way))
    my_back = (my_back * (1.0 / total_rows)).astype(bf16)
    back = exchanged(spread(my_back, count), ALL, this_way).reshape(K, width)

    landed = swapped(half_product(striped_kernel, OTHER, place, hidden, back))
    kept = half_product(striped_kernel, MINE, place, hidden, back)
    own, pieces = sum_of_halves(place, kept, landed, xs)
    my_rows, gram = rows_and_gram(place, exchanged(pieces, "x"), own, 1.0 / total_rows)
    count = 4 * xs
    gram = total(exchanged(gram.reshape(count, 3 * HALF // count, HALF), NEAR))
    gram = total(exchanged(spread(gram, zs), "z"))
    gram = total(exchanged(spread(gram, ys // 2), "y_hi"))
    gram = exchanged(spread(gram, count), NEAR).reshape(3 * HALF, HALF)
    return factor_call(gram, my_rows)


def solution(mesh):
    rows, cols = mesh.devices.shape
    side = math.isqrt(rows)
    sizes = (side, rows // side, cols // 2)
    grid = Mesh(mesh.devices.reshape(side // 2, 2, *sizes[1:], 2), ALL)
    in_specs = (P(ROW, COL), P(COL, None))
    out_specs = (P(ALL, None), P())
    return jax.shard_map(
        lambda *args: body(sizes, *args), mesh=grid, in_specs=in_specs, out_specs=out_specs, check_vma=False
    )
```

```python
import math

import jax
import jax.numpy as jnp
from jax import lax
from jax.experimental import pallas as pl
from jax.experimental.pallas import tpu as pltpu
from jax.sharding import Mesh, PartitionSpec as P

D = 7168
K = 256
HALF = K // 2
HIGH = lax.Precision.HIGHEST

def dot(a, b, over_a=1, over_b=0, precision=None):
    return lax.dot_general(
        a, b, (((over_a,), (over_b,)), ((), ())), precision=precision, preferred_element_type=jnp.float32
    )


def terms(a):
    high = a.astype(jnp.bfloat16)
    return high, (a - high.astype(jnp.float32)).astype(jnp.bfloat16)


def factor_kernel(packed_ref, rows_ref, basis_ref, factor_ref, gram_ref, g_ref, x_ref, work_ref):
    bf16 = jnp.bfloat16
    corner = packed_ref[HALF : 2 * HALF, :]
    gram_ref[:HALF, :HALF] = packed_ref[:HALF, :]
    gram_ref[:HALF, HALF:] = corner
    gram_ref[HALF:, :HALF] = corner.T
    gram_ref[HALF:, HALF:] = packed_ref[2 * HALF :, :]
    row = lax.broadcasted_iota(jnp.int32, (K, K), 0)
    col = lax.broadcasted_iota(jnp.int32, (K, K), 1)
    eye = (row == col).astype(jnp.float32)
    upper = jnp.where(row < col, 1.0, jnp.where(row == col, 0.5, 0.0))
    on_diag = jnp.where(row == col, gram_ref[...], 0.0)
    s_row = lax.rsqrt(jnp.sum(on_diag, axis=0, keepdims=True))
    s_col = lax.rsqrt(jnp.sum(on_diag, axis=1, keepdims=True))

    def change_for(g):
        f = (g - eye) * upper
        fb = f.astype(bf16)
        a = f - dot(fb, fb, 0, 0) * upper
        ab = a.astype(bf16)
        return (dot(ab, ab) - a).astype(bf16)

    def moved(g, n):
        y = g + sum(dot(part, n) for part in terms(g))
        return y + sum(dot(n, part, 0, 0) for part in terms(y))

    def size(e):
        return jnp.sum(e * e)

    g = gram_ref[...] * s_row * s_col
    n = change_for(g)
    x_ref[...] = s_col * (eye + n.astype(jnp.float32))
    g_ref[...] = moved(g, n)

    def step(state):
        count, _ = state
        g = g_ref[...]
        n = change_for(g)
        g = moved(g, n)
        g_ref[...] = g
        x = x_ref[...]
        x_ref[...] = x + sum(dot(part, n) for part in terms(x))
        return count + 1, size(g - eye)

    def more(state):
        count, err = state
        return jnp.logical_and(count < 12, err > 1e-5)

    _, err = lax.while_loop(more, step, (jnp.int32(0), jnp.float32(1.0)))
    ok = err <= 1e-5

    @pl.when(ok)
    def _():
        x = x_ref[...]
        last = ((g_ref[...] - eye) * upper).astype(bf16)
        x_ref[...] = x - dot(x.astype(bf16), last)

    @pl.when(jnp.logical_not(ok))
    def _():
        work_ref[:, :K] = gram_ref[...]
        work_ref[:, K:] = eye
        lane = lax.broadcasted_iota(jnp.int32, (1, 2 * K), 1)

        def eliminate(k, carry):
            line = work_ref[pl.ds(k, 1), :]
            pivot = jnp.sum(jnp.where(lane == k, line, 0.0), axis=1, keepdims=True)
            line = line * lax.rsqrt(pivot)
            coef = jnp.where(lane[:, :K] > k, line[:, :K], 0.0)
            work_ref[...] = work_ref[...] - dot(coef, line, 0, 0, HIGH)
            work_ref[pl.ds(k, 1), :] = line
            return carry

        lax.fori_loop(0, K, eliminate, 0)
        x_ref[...] = work_ref[:, K:].T

    x = jnp.where(row <= col, x_ref[...], 0.0)
    basis_ref[...] = dot(rows_ref[...], x, precision=HIGH)
    factor_ref[...] = jnp.where(row <= col, dot(x, gram_ref[...], 0, 0, HIGH), 0.0)


def factor_call(packed, rows):
    square = pltpu.VMEM((K, K), jnp.float32)
    return pl.pallas_call(
        factor_kernel,
        out_shape=(jax.ShapeDtypeStruct(rows.shape, jnp.float32), jax.ShapeDtypeStruct((K, K), jnp.float32)),
        in_specs=[WHOLE] * 2,
        out_specs=(WHOLE, WHOLE),
        scratch_shapes=[square, square, square, pltpu.VMEM((K, 2 * K), jnp.float32)],
        compiler_params=PARAMS,
        name="factor",
    )(packed, rows)


WHOLE = pl.BlockSpec(memory_space=pltpu.VMEM)
PARAMS = pltpu.CompilerParams(vmem_limit_bytes=12 * 1024 * 1024)


def opening_kernel(half_ref, x_ref, hidden_ref, right_ref, send_ref, hidden_out, right_out, sems):
    rows = send_ref.shape[0]
    halves = [pl.ds(pl.multiple_of(half * rows, rows), rows) for half in (half_ref[0], 1 - half_ref[0])]
    copies = [
        pltpu.make_async_copy(right_ref, right_out, sems.at[0]),
        pltpu.make_async_copy(hidden_ref.at[halves[0], :], hidden_out.at[halves[0], :], sems.at[1]),
        pltpu.make_async_copy(hidden_ref.at[halves[1], :], hidden_out.at[halves[1], :], sems.at[2]),
    ]
    for copy in copies:
        copy.start()
    copies[0].wait()
    copies[1].wait()
    send_ref[...] = dot(hidden_out[halves[0], :], right_out[...]).astype(send_ref.dtype)
    copies[2].wait()


def opening(half, x, hidden, right):
    return pl.pallas_call(
        opening_kernel,
        out_shape=(
            pltpu.VMEM((hidden.shape[0] // 2, K), jnp.bfloat16),
            pltpu.VMEM(hidden.shape, hidden.dtype),
            pltpu.VMEM(right.shape, right.dtype),
        ),
        in_specs=[SCALAR, SCALAR, *[pl.BlockSpec(memory_space=pltpu.HBM)] * 2],
        out_specs=(WHOLE, WHOLE, WHOLE),
        scratch_shapes=[pltpu.SemaphoreType.DMA((3,))],
        compiler_params=pltpu.CompilerParams(vmem_limit_bytes=12 * 1024 * 1024),
        name="opening",
    )(half, x, pltpu.with_memory_space_constraint(hidden, pltpu.HBM), pltpu.with_memory_space_constraint(right, pltpu.HBM))


SCALAR = pl.BlockSpec(memory_space=pltpu.SMEM)


def half_kernel(half_ref, hidden_ref, right_ref, out_ref):
    rows = out_ref.shape[0]
    out_ref[...] = dot(hidden_ref[pl.ds(pl.multiple_of(half_ref[0] * rows, rows), rows), :], right_ref[...])


def striped_kernel(half_ref, hidden_ref, back_ref, out_ref):
    rows = out_ref.shape[0]
    tile = rows // 4
    blocks = [hidden_ref[pl.ds(pl.multiple_of((2 * i + half_ref[0]) * tile, tile), tile), :] for i in range(4)]
    out_ref[...] = dot(jnp.concatenate(blocks, axis=0), back_ref[...], 1, 1)


def half_product(kernel, half, hidden, right):
    return pl.pallas_call(
        kernel,
        out_shape=pltpu.VMEM((hidden.shape[0] // 2, K), jnp.float32),
        in_specs=[SCALAR, WHOLE, WHOLE],
        out_specs=WHOLE,
        compiler_params=PARAMS,
        name="half_product",
    )(half, hidden, right)


def back_kernel(half_ref, hidden_ref, first_ref, *refs):
    *so_far, out_ref = refs
    rows = first_ref.shape[0]
    part = dot(first_ref[...], hidden_ref[pl.ds(pl.multiple_of(half_ref[0] * rows, rows), rows), :], 0, 0)
    for ref in so_far:
        part = part + ref[...]
    out_ref[...] = part.astype(out_ref.dtype)


def half_back(half, hidden, first, dtype, *so_far):
    return pl.pallas_call(
        back_kernel,
        out_shape=jax.ShapeDtypeStruct((K, hidden.shape[1]), dtype),
        in_specs=[SCALAR, *[WHOLE] * (2 + len(so_far))],
        out_specs=WHOLE,
        compiler_params=PARAMS,
        name="half_back",
    )(half, hidden, first, *so_far)


def sum_kernel(x_ref, kept_ref, landed_ref, own_ref, pieces_ref):
    count, tile, _ = pieces_ref.shape
    own = pl.ds(pl.multiple_of(x_ref[0] * tile, tile), tile)
    own_ref[...] = kept_ref[own, :] + landed_ref[own, :]
    for i in range(count):
        block = slice(i * tile, (i + 1) * tile)
        pieces_ref[i] = (kept_ref[block, :] + landed_ref[block, :]).astype(pieces_ref.dtype)


def sum_of_halves(x, kept, landed, count):
    tile = kept.shape[0] // count
    return pl.pallas_call(
        sum_kernel,
        out_shape=(
            jax.ShapeDtypeStruct((tile, K), jnp.float32),
            jax.ShapeDtypeStruct((count, tile, K), jnp.bfloat16),
        ),
        in_specs=[SCALAR, WHOLE, WHOLE],
        out_specs=(WHOLE, WHOLE),
        compiler_params=PARAMS,
        name="sum_of_halves",
    )(x, kept, pltpu.with_memory_space_constraint(landed, pltpu.VMEM))


def gram_kernel(scale, x_ref, landed_ref, own_ref, rows_ref, packed_ref):
    rows = own_ref[...]
    for i in range(landed_ref.shape[0]):
        rows = rows + jnp.where(x_ref[0] == i, 0.0, landed_ref[i].astype(jnp.float32))
    rows_ref[...] = rows
    left, right = rows[:, :HALF], rows[:, HALF:]
    packed_ref[:HALF, :] = dot(left, left, 0, 0, HIGH) * scale
    packed_ref[HALF : 2 * HALF, :] = dot(left, right, 0, 0, HIGH) * scale
    packed_ref[2 * HALF :, :] = dot(right, right, 0, 0, HIGH) * scale


def rows_and_gram(x, landed, own, scale):
    return pl.pallas_call(
        lambda *refs: gram_kernel(scale, *refs),
        out_shape=(
            jax.ShapeDtypeStruct(landed.shape[1:], jnp.float32),
            jax.ShapeDtypeStruct((3 * HALF, HALF), jnp.float32),
        ),
        in_specs=[SCALAR, WHOLE, WHOLE],
        out_specs=(WHOLE, WHOLE),
        compiler_params=PARAMS,
        name="rows_and_gram",
    )(x, landed, own)


ROW = ("y_hi", "y_lo", "z")
COL = ("x", "core")
NEAR = ("y_lo", *COL)
ALL = (*ROW, *COL)


def swapped(block):
    return lax.ppermute(block, "core", [(0, 1), (1, 0)])


def line_groups(sizes, along):
    ys, zs, xs = sizes
    groups = []
    for core in range(2):
        y_steps, z_steps = along[core]
        for y in range(ys):
            for z in range(zs):
                if any(y // s % n for s, n in y_steps) or any(z // s % n for s, n in z_steps):
                    continue
                spots = [(y, z)]
                for s, n in y_steps:
                    spots = [(a + s * k, b) for a, b in spots for k in range(n)]
                for s, n in z_steps:
                    spots = [(a, b + s * k) for a, b in spots for k in range(n)]
                for x in range(xs):
                    groups.append([((a * zs + b) * xs + x) * 2 + core for a, b in spots])
    return groups


def exchanged(pieces, axis, groups=None):
    return lax.all_to_all(pieces, axis, 0, 0, axis_index_groups=groups)


def spread(block, count):
    return jnp.broadcast_to(block[None], (count, *block.shape))


def total(pieces):
    return jnp.sum(pieces.astype(jnp.float32), axis=0)


def body(sizes, hidden, test_matrix):
    bf16 = jnp.bfloat16
    tok_rows, width = hidden.shape
    tile = tok_rows // 8
    ys, zs, xs = sizes
    total_rows = tok_rows * ys * zs
    core = lax.axis_index("core")
    mine, other, x = core.reshape(1), (1 - core).reshape(1), lax.axis_index("x").reshape(1)

    send, hidden, test_matrix = opening(other, x, hidden, test_matrix)
    landed = swapped(send)
    pieces = (half_product(half_kernel, mine, hidden, test_matrix) + landed).astype(bf16).reshape(xs, tile, K)
    my_first = (total(exchanged(pieces, "x")) * (1.0 / math.sqrt(D))).astype(bf16)
    my_half = exchanged(spread(my_first, xs), "x").reshape(tok_rows // 2, K)
    other_half = swapped(my_half)
    local_back = half_back(mine, hidden, my_half, jnp.float32)
    local_back = half_back(other, hidden, other_half, bf16, local_back)

    lines = ((), ((1, zs),)), (((1, ys),), ())
    this_way, that_way = line_groups(sizes, lines), line_groups(sizes, lines[::-1])
    count = len(this_way[0])
    pieces = local_back.reshape(count, K // count, width)
    my_back = total(exchanged(pieces, ALL, this_way)).astype(bf16)
    my_back = total(exchanged(spread(my_back, len(that_way[0])), ALL, that_way))
    my_back = (my_back * (1.0 / total_rows)).astype(bf16)
    back = exchanged(spread(my_back, count), ALL, this_way).reshape(K, width)

    landed = swapped(half_product(striped_kernel, other, hidden, back))
    kept = half_product(striped_kernel, mine, hidden, back)
    own, pieces = sum_of_halves(x, kept, landed, xs)
    my_rows, gram = rows_and_gram(x, exchanged(pieces, "x"), own, 1.0 / total_rows)
    count = 4 * xs
    gram = total(exchanged(gram.reshape(count, 3 * HALF // count, HALF), NEAR))
    gram = total(exchanged(spread(gram, zs), "z"))
    gram = total(exchanged(spread(gram, ys // 2), "y_hi"))
    gram = exchanged(spread(gram, count), NEAR).reshape(3 * HALF, HALF)
    return factor_call(gram, my_rows)


def solution(mesh):
    rows, cols = mesh.devices.shape
    side = math.isqrt(rows)
    sizes = (side, rows // side, cols // 2)
    grid = Mesh(mesh.devices.reshape(side // 2, 2, *sizes[1:], 2), ALL)
    in_specs = (P(ROW, COL), P(COL, None))
    out_specs = (P(ALL, None), P())
    return jax.shard_map(
        lambda *args: body(sizes, *args), mesh=grid, in_specs=in_specs, out_specs=out_specs, check_vma=False
    )
```

```python
import math

import jax
import jax.numpy as jnp
from jax import lax
from jax.experimental import pallas as pl
from jax.experimental.pallas import tpu as pltpu
from jax.sharding import Mesh, PartitionSpec as P

D = 7168
K = 256
HALF = K // 2
HIGH = lax.Precision.HIGHEST

def dot(a, b, over_a=1, over_b=0, precision=None):
    return lax.dot_general(
        a, b, (((over_a,), (over_b,)), ((), ())), precision=precision, preferred_element_type=jnp.float32
    )


def terms(a):
    high = a.astype(jnp.bfloat16)
    return high, (a - high.astype(jnp.float32)).astype(jnp.bfloat16)


def factor_kernel(packed_ref, rows_ref, basis_ref, factor_ref, gram_ref, g_ref, x_ref, work_ref):
    bf16 = jnp.bfloat16
    corner = packed_ref[HALF : 2 * HALF, :]
    gram_ref[:HALF, :HALF] = packed_ref[:HALF, :]
    gram_ref[:HALF, HALF:] = corner
    gram_ref[HALF:, :HALF] = corner.T
    gram_ref[HALF:, HALF:] = packed_ref[2 * HALF :, :]
    row = lax.broadcasted_iota(jnp.int32, (K, K), 0)
    col = lax.broadcasted_iota(jnp.int32, (K, K), 1)
    eye = (row == col).astype(jnp.float32)
    upper = jnp.where(row < col, 1.0, jnp.where(row == col, 0.5, 0.0))
    on_diag = jnp.where(row == col, gram_ref[...], 0.0)
    s_row = lax.rsqrt(jnp.sum(on_diag, axis=0, keepdims=True))
    s_col = lax.rsqrt(jnp.sum(on_diag, axis=1, keepdims=True))

    def change_for(g):
        f = (g - eye) * upper
        fb = f.astype(bf16)
        a = f - dot(fb, fb, 0, 0) * upper
        ab = a.astype(bf16)
        return (dot(ab, ab) - a).astype(bf16)

    def moved(g, n):
        y = g + sum(dot(part, n) for part in terms(g))
        return y + sum(dot(n, part, 0, 0) for part in terms(y))

    def size(e):
        return jnp.sum(e * e)

    g = gram_ref[...] * s_row * s_col
    n = change_for(g)
    x_ref[...] = s_col * (eye + n.astype(jnp.float32))
    g_ref[...] = moved(g, n)

    def step(state):
        count, _ = state
        g = g_ref[...]
        n = change_for(g)
        g = moved(g, n)
        g_ref[...] = g
        x = x_ref[...]
        x_ref[...] = x + sum(dot(part, n) for part in terms(x))
        return count + 1, size(g - eye)

    def more(state):
        count, err = state
        return jnp.logical_and(count < 12, err > 1e-5)

    _, err = lax.while_loop(more, step, (jnp.int32(0), jnp.float32(1.0)))
    ok = err <= 1e-5

    @pl.when(ok)
    def _():
        x = x_ref[...]
        last = ((g_ref[...] - eye) * upper).astype(bf16)
        x_ref[...] = x - dot(x.astype(bf16), last)

    @pl.when(jnp.logical_not(ok))
    def _():
        work_ref[:, :K] = gram_ref[...]
        work_ref[:, K:] = eye
        lane = lax.broadcasted_iota(jnp.int32, (1, 2 * K), 1)

        def eliminate(k, carry):
            line = work_ref[pl.ds(k, 1), :]
            pivot = jnp.sum(jnp.where(lane == k, line, 0.0), axis=1, keepdims=True)
            line = line * lax.rsqrt(pivot)
            coef = jnp.where(lane[:, :K] > k, line[:, :K], 0.0)
            work_ref[...] = work_ref[...] - dot(coef, line, 0, 0, HIGH)
            work_ref[pl.ds(k, 1), :] = line
            return carry

        lax.fori_loop(0, K, eliminate, 0)
        x_ref[...] = work_ref[:, K:].T

    x = jnp.where(row <= col, x_ref[...], 0.0)
    basis_ref[...] = dot(rows_ref[...], x, precision=HIGH)
    factor_ref[...] = jnp.where(row <= col, dot(x, gram_ref[...], 0, 0, HIGH), 0.0)


def factor_call(packed, rows):
    square = pltpu.VMEM((K, K), jnp.float32)
    return pl.pallas_call(
        factor_kernel,
        out_shape=(jax.ShapeDtypeStruct(rows.shape, jnp.float32), jax.ShapeDtypeStruct((K, K), jnp.float32)),
        in_specs=[WHOLE] * 2,
        out_specs=(WHOLE, WHOLE),
        scratch_shapes=[square, square, square, pltpu.VMEM((K, 2 * K), jnp.float32)],
        compiler_params=PARAMS,
        name="factor",
    )(packed, rows)


WHOLE = pl.BlockSpec(memory_space=pltpu.VMEM)
PARAMS = pltpu.CompilerParams(vmem_limit_bytes=12 * 1024 * 1024)


SCALAR = pl.BlockSpec(memory_space=pltpu.SMEM)
STEPS = 8


def opening_kernel(core_ref, me_ref, hidden_ref, right_ref, send_ref, keep_ref, hidden_out, right_buf, sems):
    rows = hidden_out.shape[0] // STEPS
    blocks = [slice(i * rows, (i + 1) * rows) for i in range(STEPS)]
    copies = [pltpu.make_async_copy(right_ref, right_buf, sems.at[STEPS])]
    for i, block in enumerate(blocks):
        copies.append(pltpu.make_async_copy(hidden_ref.at[block, :], hidden_out.at[block, :], sems.at[i]))
    for copy in copies:
        copy.start()
    for copy in copies:
        copy.wait()
    first = dot(hidden_out[...], right_buf[...])
    left, right = first[:, :HALF], first[:, HALF:]
    send_ref[...] = jnp.where(core_ref[0] == 0, right, left).astype(send_ref.dtype)
    keep_ref[...] = jnp.where(core_ref[0] == 0, left, right)


def opening(core, me, hidden, right):
    rows = hidden.shape[0]
    in_hbm = pl.BlockSpec(memory_space=pltpu.HBM)
    return pl.pallas_call(
        opening_kernel,
        out_shape=(
            jax.ShapeDtypeStruct((rows, HALF), jnp.bfloat16),
            jax.ShapeDtypeStruct((rows, HALF), jnp.float32),
            jax.ShapeDtypeStruct(hidden.shape, hidden.dtype),
        ),
        in_specs=[SCALAR, SCALAR, in_hbm, in_hbm],
        out_specs=(WHOLE, WHOLE, WHOLE),
        scratch_shapes=[pltpu.VMEM(right.shape, right.dtype), pltpu.SemaphoreType.DMA((STEPS + 1,))],
        compiler_params=PARAMS,
        name="opening",
    )(
        core,
        me,
        pltpu.with_memory_space_constraint(hidden, pltpu.HBM),
        pltpu.with_memory_space_constraint(right, pltpu.HBM),
    )


def pieces_kernel(own_ref, landed_ref, hidden_ref, pieces_ref, _):
    count, tile, _ = pieces_ref.shape
    for i in range(count):
        block = slice(i * tile, (i + 1) * tile)
        pieces_ref[i] = (own_ref[block, :] + landed_ref[block, :].astype(jnp.float32)).astype(pieces_ref.dtype)


def first_pieces(own, landed, hidden, count):
    return pl.pallas_call(
        pieces_kernel,
        out_shape=(
            jax.ShapeDtypeStruct((count, own.shape[0] // count, HALF), jnp.bfloat16),
            jax.ShapeDtypeStruct(hidden.shape, hidden.dtype),
        ),
        in_specs=[WHOLE] * 3,
        out_specs=(WHOLE, WHOLE),
        input_output_aliases={2: 1},
        compiler_params=PARAMS,
        name="first_pieces",
    )(own, landed, hidden)


def back_kernel(first_ref, own_ref, pair_ref, out_ref):
    first = first_ref[...]
    out_ref[:HALF, :] = dot(first, own_ref[...], 0, 0).astype(out_ref.dtype)
    out_ref[HALF:, :] = dot(first, pair_ref[...], 0, 0).astype(out_ref.dtype)


def local_backs(first, own, pair):
    return pl.pallas_call(
        back_kernel,
        out_shape=jax.ShapeDtypeStruct((K, own.shape[1]), jnp.bfloat16),
        in_specs=[WHOLE] * 3,
        out_specs=WHOLE,
        compiler_params=PARAMS,
        name="local_backs",
    )(first, own, pair)


def sketch_kernel(me_ref, own_ref, pair_ref, back_ref, mine_ref, pieces_ref):
    count, tile, _ = pieces_ref.shape
    sketch = dot(own_ref[...], back_ref[:HALF, :], 1, 1) + dot(pair_ref[...], back_ref[HALF:, :], 1, 1)
    for i in range(count):
        block = sketch[i * tile : (i + 1) * tile, :]
        pieces_ref[i] = block.astype(pieces_ref.dtype)

        @pl.when(me_ref[0] == i)
        def _():
            mine_ref[...] = block


def sketch_pieces(me, own, pair, back, count):
    tile = own.shape[0] // count
    return pl.pallas_call(
        sketch_kernel,
        out_shape=(
            jax.ShapeDtypeStruct((tile, HALF), jnp.float32),
            jax.ShapeDtypeStruct((count, tile, HALF), jnp.bfloat16),
        ),
        in_specs=[SCALAR, WHOLE, WHOLE, WHOLE],
        out_specs=(WHOLE, WHOLE),
        compiler_params=PARAMS,
        name="sketch_pieces",
    )(me, own, pair, back)


def gram_kernel(scale, me_ref, landed_ref, own_ref, rows_ref, packed_ref):
    halves = []
    for half in range(2):
        parts = [
            jnp.where(me_ref[0] == i, own_ref[...], landed_ref[i].astype(jnp.float32))
            for i in range(half, landed_ref.shape[0], 2)
        ]
        halves.append(sum(parts[1:], parts[0]))
    left, right = halves
    rows_ref[:, :HALF] = left
    rows_ref[:, HALF:] = right
    packed_ref[:HALF, :] = dot(left, left, 0, 0, HIGH) * scale
    packed_ref[HALF : 2 * HALF, :] = dot(left, right, 0, 0, HIGH) * scale
    packed_ref[2 * HALF :, :] = dot(right, right, 0, 0, HIGH) * scale


def rows_and_gram(me, landed, own, scale):
    return pl.pallas_call(
        lambda *refs: gram_kernel(scale, *refs),
        out_shape=(
            jax.ShapeDtypeStruct((own.shape[0], K), jnp.float32),
            jax.ShapeDtypeStruct((3 * HALF, HALF), jnp.float32),
        ),
        in_specs=[SCALAR, WHOLE, WHOLE],
        out_specs=(WHOLE, WHOLE),
        compiler_params=PARAMS,
        name="rows_and_gram",
    )(me, landed, own)


ROW = ("y_hi", "y_lo", "z")
COL = ("x", "core")
NEAR = ("y_lo", *COL)
ALL = (*ROW, *COL)


def swapped(block):
    return lax.ppermute(block, "core", [(0, 1), (1, 0)])


def line_groups(sizes, along):
    ys, zs, xs = sizes
    groups = []
    for core in range(2):
        y_steps, z_steps = along[core]
        for y in range(ys):
            for z in range(zs):
                if any(y // s % n for s, n in y_steps) or any(z // s % n for s, n in z_steps):
                    continue
                spots = [(y, z)]
                for s, n in y_steps:
                    spots = [(a + s * k, b) for a, b in spots for k in range(n)]
                for s, n in z_steps:
                    spots = [(a, b + s * k) for a, b in spots for k in range(n)]
                for x in range(xs):
                    groups.append([((a * zs + b) * xs + x) * 2 + core for a, b in spots])
    return groups


def exchanged(pieces, axis, groups=None):
    return lax.all_to_all(pieces, axis, 0, 0, axis_index_groups=groups)


def spread(block, count):
    return jnp.broadcast_to(block[None], (count, *block.shape))


def total(pieces):
    return jnp.sum(pieces.astype(jnp.float32), axis=0)


def body(sizes, hidden, test_matrix):
    bf16 = jnp.bfloat16
    tok_rows, width = hidden.shape
    ys, zs, xs = sizes
    total_rows = tok_rows * ys * zs
    core, me = (lax.axis_index(axis).reshape(1) for axis in ("core", COL))

    send, keep, hidden = opening(core, me, hidden, test_matrix)
    pieces, hidden = first_pieces(keep, swapped(send), hidden, xs)
    pair = swapped(hidden)
    first = (total(exchanged(pieces, "x")) * (1.0 / math.sqrt(D))).astype(bf16)
    first = exchanged(spread(first, xs), "x").reshape(tok_rows, HALF)
    local_back = local_backs(first, hidden, pair)

    lines = ((), ((1, zs),)), (((1, ys),), ())
    this_way, that_way = line_groups(sizes, lines), line_groups(sizes, lines[::-1])
    count = len(this_way[0])
    pieces = local_back.reshape(count, K // count, width)
    my_back = total(exchanged(pieces, ALL, this_way)).astype(bf16)
    my_back = total(exchanged(spread(my_back, len(that_way[0])), ALL, that_way))
    my_back = (my_back * (1.0 / total_rows)).astype(bf16)
    back = exchanged(spread(my_back, count), ALL, this_way).reshape(K, width)

    own, pieces = sketch_pieces(me, hidden, pair, back, 2 * xs)
    my_rows, gram = rows_and_gram(me, exchanged(pieces, COL), own, 1.0 / total_rows)
    count = 4 * xs
    gram = total(exchanged(gram.reshape(count, 3 * HALF // count, HALF), NEAR))
    gram = total(exchanged(spread(gram, zs), "z"))
    gram = total(exchanged(spread(gram, ys // 2), "y_hi"))
    gram = exchanged(spread(gram, count), NEAR).reshape(3 * HALF, HALF)
    return factor_call(gram, my_rows)


def solution(mesh):
    rows, cols = mesh.devices.shape
    side = math.isqrt(rows)
    sizes = (side, rows // side, cols // 2)
    grid = Mesh(mesh.devices.reshape(side // 2, 2, *sizes[1:], 2), ALL)
    in_specs = (P(ROW, COL), P(COL, None))
    out_specs = (P(ALL, None), P())
    return jax.shard_map(
        lambda *args: body(sizes, *args), mesh=grid, in_specs=in_specs, out_specs=out_specs, check_vma=False
    )
```

```python
import math

import jax
import jax.numpy as jnp
from jax import lax
from jax.experimental import pallas as pl
from jax.experimental.pallas import tpu as pltpu
from jax.sharding import Mesh, PartitionSpec as P

D = 7168
K = 256
HALF = K // 2
HIGH = lax.Precision.HIGHEST

def dot(a, b, over_a=1, over_b=0, precision=None):
    return lax.dot_general(
        a, b, (((over_a,), (over_b,)), ((), ())), precision=precision, preferred_element_type=jnp.float32
    )


def terms(a):
    high = a.astype(jnp.bfloat16)
    return high, (a - high.astype(jnp.float32)).astype(jnp.bfloat16)


def factor_kernel(packed_ref, rows_ref, basis_ref, factor_ref, gram_ref, g_ref, x_ref, work_ref):
    bf16 = jnp.bfloat16
    corner = packed_ref[HALF : 2 * HALF, :]
    gram_ref[:HALF, :HALF] = packed_ref[:HALF, :]
    gram_ref[:HALF, HALF:] = corner
    gram_ref[HALF:, :HALF] = corner.T
    gram_ref[HALF:, HALF:] = packed_ref[2 * HALF :, :]
    row = lax.broadcasted_iota(jnp.int32, (K, K), 0)
    col = lax.broadcasted_iota(jnp.int32, (K, K), 1)
    eye = (row == col).astype(jnp.float32)
    upper = jnp.where(row < col, 1.0, jnp.where(row == col, 0.5, 0.0))
    on_diag = jnp.where(row == col, gram_ref[...], 0.0)
    s_row = lax.rsqrt(jnp.sum(on_diag, axis=0, keepdims=True))
    s_col = lax.rsqrt(jnp.sum(on_diag, axis=1, keepdims=True))

    def change_for(g):
        f = (g - eye) * upper
        fb = f.astype(bf16)
        a = f - dot(fb, fb, 0, 0) * upper
        ab = a.astype(bf16)
        return (dot(ab, ab) - a).astype(bf16)

    def moved(g, n):
        y = g + sum(dot(part, n) for part in terms(g))
        return y + sum(dot(n, part, 0, 0) for part in terms(y))

    def size(e):
        return jnp.sum(e * e)

    g = gram_ref[...] * s_row * s_col
    n = change_for(g)
    x_ref[...] = s_col * (eye + n.astype(jnp.float32))
    g_ref[...] = moved(g, n)

    def step(state):
        count, _ = state
        g = g_ref[...]
        n = change_for(g)
        g = moved(g, n)
        g_ref[...] = g
        x = x_ref[...]
        x_ref[...] = x + sum(dot(part, n) for part in terms(x))
        return count + 1, size(g - eye)

    def more(state):
        count, err = state
        return jnp.logical_and(count < 12, err > 1e-5)

    _, err = lax.while_loop(more, step, (jnp.int32(0), jnp.float32(1.0)))
    ok = err <= 1e-5

    @pl.when(ok)
    def _():
        x = x_ref[...]
        last = ((g_ref[...] - eye) * upper).astype(bf16)
        x_ref[...] = x - dot(x.astype(bf16), last)

    @pl.when(jnp.logical_not(ok))
    def _():
        work_ref[:, :K] = gram_ref[...]
        work_ref[:, K:] = eye
        lane = lax.broadcasted_iota(jnp.int32, (1, 2 * K), 1)

        def eliminate(k, carry):
            line = work_ref[pl.ds(k, 1), :]
            pivot = jnp.sum(jnp.where(lane == k, line, 0.0), axis=1, keepdims=True)
            scale = lax.rsqrt(pivot)
            line = line * (scale * (1.5 - 0.5 * pivot * scale * scale))
            coef = jnp.where(lane[:, :K] > k, line[:, :K], 0.0)
            work_ref[...] = work_ref[...] - dot(coef, line, 0, 0, HIGH)
            work_ref[pl.ds(k, 1), :] = line
            return carry

        lax.fori_loop(0, K, eliminate, 0)
        x_ref[...] = work_ref[:, K:].T

    x = jnp.where(row <= col, x_ref[...], 0.0)
    basis_ref[...] = dot(rows_ref[...], x, precision=HIGH)
    factor_ref[...] = jnp.where(row <= col, dot(x, gram_ref[...], 0, 0, HIGH), 0.0)


def factor_call(packed, rows):
    square = pltpu.VMEM((K, K), jnp.float32)
    return pl.pallas_call(
        factor_kernel,
        out_shape=(jax.ShapeDtypeStruct(rows.shape, jnp.float32), jax.ShapeDtypeStruct((K, K), jnp.float32)),
        in_specs=[WHOLE] * 2,
        out_specs=(WHOLE, WHOLE),
        scratch_shapes=[square, square, square, pltpu.VMEM((K, 2 * K), jnp.float32)],
        compiler_params=PARAMS,
        name="factor",
    )(packed, rows)


WHOLE = pl.BlockSpec(memory_space=pltpu.VMEM)
PARAMS = pltpu.CompilerParams(vmem_limit_bytes=12 * 1024 * 1024)


SCALAR = pl.BlockSpec(memory_space=pltpu.SMEM)
STEPS = 8


def half_columns(core_ref):
    return pl.ds(pl.multiple_of(core_ref[0] * HALF, HALF), HALF)


def opening_kernel(core_ref, me_ref, hidden_ref, right_ref, first_ref, hidden_out, right_buf, sems):
    rows = hidden_out.shape[0] // STEPS
    blocks = [slice(i * rows, (i + 1) * rows) for i in range(STEPS)]
    copies = [pltpu.make_async_copy(right_ref, right_buf, sems.at[STEPS])]
    for i, block in enumerate(blocks):
        copies.append(pltpu.make_async_copy(hidden_ref.at[block, :], hidden_out.at[block, :], sems.at[i]))
    for copy in copies:
        copy.start()
    for copy in copies:
        copy.wait()
    first_ref[...] = dot(hidden_out[...], right_buf[:, half_columns(core_ref)])


def opening(core, me, hidden, right):
    in_hbm = pl.BlockSpec(memory_space=pltpu.HBM)
    return pl.pallas_call(
        opening_kernel,
        out_shape=(
            jax.ShapeDtypeStruct((hidden.shape[0], HALF), jnp.float32),
            jax.ShapeDtypeStruct(hidden.shape, hidden.dtype),
        ),
        in_specs=[SCALAR, SCALAR, in_hbm, in_hbm],
        out_specs=(WHOLE, WHOLE),
        scratch_shapes=[pltpu.VMEM(right.shape, right.dtype), pltpu.SemaphoreType.DMA((STEPS + 1,))],
        compiler_params=PARAMS,
        name="opening",
    )(
        core,
        me,
        pltpu.with_memory_space_constraint(hidden, pltpu.HBM),
        pltpu.with_memory_space_constraint(right, pltpu.HBM),
    )


def pieces_kernel(core_ref, own_ref, pair_ref, right_ref, pieces_ref):
    count, tile, _ = pieces_ref.shape
    first = own_ref[...] + dot(pair_ref[...], right_ref[:, half_columns(core_ref)])
    for i in range(count):
        pieces_ref[i] = first[i * tile : (i + 1) * tile, :].astype(pieces_ref.dtype)


def first_pieces(core, own, pair, right, count):
    return pl.pallas_call(
        pieces_kernel,
        out_shape=jax.ShapeDtypeStruct((count, own.shape[0] // count, HALF), jnp.bfloat16),
        in_specs=[SCALAR, WHOLE, WHOLE, WHOLE],
        out_specs=WHOLE,
        compiler_params=PARAMS,
        name="first_pieces",
    )(core, own, pair, right)


def back_kernel(first_ref, own_ref, pair_ref, out_ref):
    first = first_ref[...]
    out_ref[:HALF, :] = dot(first, own_ref[...], 0, 0).astype(out_ref.dtype)
    out_ref[HALF:, :] = dot(first, pair_ref[...], 0, 0).astype(out_ref.dtype)


def local_backs(first, own, pair):
    return pl.pallas_call(
        back_kernel,
        out_shape=jax.ShapeDtypeStruct((K, own.shape[1]), jnp.bfloat16),
        in_specs=[WHOLE] * 3,
        out_specs=WHOLE,
        compiler_params=PARAMS,
        name="local_backs",
    )(first, own, pair)


def sketch_kernel(me_ref, own_ref, pair_ref, back_ref, mine_ref, pieces_ref):
    count, tile, _ = pieces_ref.shape
    sketch = dot(own_ref[...], back_ref[:HALF, :], 1, 1) + dot(pair_ref[...], back_ref[HALF:, :], 1, 1)
    for i in range(count):
        block = sketch[i * tile : (i + 1) * tile, :]
        pieces_ref[i] = block.astype(pieces_ref.dtype)

        @pl.when(me_ref[0] == i)
        def _():
            mine_ref[...] = block


def sketch_pieces(me, own, pair, back, count):
    tile = own.shape[0] // count
    return pl.pallas_call(
        sketch_kernel,
        out_shape=(
            jax.ShapeDtypeStruct((tile, HALF), jnp.float32),
            jax.ShapeDtypeStruct((count, tile, HALF), jnp.bfloat16),
        ),
        in_specs=[SCALAR, WHOLE, WHOLE, WHOLE],
        out_specs=(WHOLE, WHOLE),
        compiler_params=PARAMS,
        name="sketch_pieces",
    )(me, own, pair, back)


def gram_kernel(scale, me_ref, landed_ref, own_ref, rows_ref, packed_ref):
    halves = []
    for half in range(2):
        parts = [
            jnp.where(me_ref[0] == i, own_ref[...], landed_ref[i].astype(jnp.float32))
            for i in range(half, landed_ref.shape[0], 2)
        ]
        halves.append(sum(parts[1:], parts[0]))
    left, right = halves
    rows_ref[:, :HALF] = left
    rows_ref[:, HALF:] = right
    packed_ref[:HALF, :] = dot(left, left, 0, 0, HIGH) * scale
    packed_ref[HALF : 2 * HALF, :] = dot(left, right, 0, 0, HIGH) * scale
    packed_ref[2 * HALF :, :] = dot(right, right, 0, 0, HIGH) * scale


def rows_and_gram(me, landed, own, scale):
    return pl.pallas_call(
        lambda *refs: gram_kernel(scale, *refs),
        out_shape=(
            jax.ShapeDtypeStruct((own.shape[0], K), jnp.float32),
            jax.ShapeDtypeStruct((3 * HALF, HALF), jnp.float32),
        ),
        in_specs=[SCALAR, WHOLE, WHOLE],
        out_specs=(WHOLE, WHOLE),
        compiler_params=PARAMS,
        name="rows_and_gram",
    )(me, landed, own)


ROW = ("y_hi", "y_lo", "z")
COL = ("x", "core")
NEAR = ("y_lo", *COL)
ALL = (*ROW, *COL)


def swapped(block):
    return lax.ppermute(block, "core", [(0, 1), (1, 0)])


def line_groups(sizes, along):
    ys, zs, xs = sizes
    groups = []
    for core in range(2):
        y_steps, z_steps = along[core]
        for y in range(ys):
            for z in range(zs):
                if any(y // s % n for s, n in y_steps) or any(z // s % n for s, n in z_steps):
                    continue
                spots = [(y, z)]
                for s, n in y_steps:
                    spots = [(a + s * k, b) for a, b in spots for k in range(n)]
                for s, n in z_steps:
                    spots = [(a, b + s * k) for a, b in spots for k in range(n)]
                for x in range(xs):
                    groups.append([((a * zs + b) * xs + x) * 2 + core for a, b in spots])
    return groups


def exchanged(pieces, axis, groups=None):
    return lax.all_to_all(pieces, axis, 0, 0, axis_index_groups=groups)


def spread(block, count):
    return jnp.broadcast_to(block[None], (count, *block.shape))


def total(pieces):
    return jnp.sum(pieces.astype(jnp.float32), axis=0)


def body(sizes, hidden, test_matrix):
    bf16 = jnp.bfloat16
    tok_rows, width = hidden.shape
    ys, zs, xs = sizes
    total_rows = tok_rows * ys * zs
    core, me = (lax.axis_index(axis).reshape(1) for axis in ("core", COL))

    pair, right = swapped(hidden), swapped(test_matrix)
    own, hidden = opening(core, me, hidden, test_matrix)
    pieces = first_pieces(core, own, pair, right, xs)
    first = (total(exchanged(pieces, "x")) * (1.0 / math.sqrt(D))).astype(bf16)
    first = exchanged(spread(first, xs), "x").reshape(tok_rows, HALF)
    local_back = local_backs(first, hidden, pair)

    lines = ((), ((1, zs),)), (((1, ys),), ())
    this_way, that_way = line_groups(sizes, lines), line_groups(sizes, lines[::-1])
    count = len(this_way[0])
    pieces = local_back.reshape(count, K // count, width)
    my_back = total(exchanged(pieces, ALL, this_way)).astype(bf16)
    my_back = total(exchanged(spread(my_back, len(that_way[0])), ALL, that_way))
    my_back = (my_back * (1.0 / total_rows)).astype(bf16)
    back = exchanged(spread(my_back, count), ALL, this_way).reshape(K, width)

    own, pieces = sketch_pieces(me, hidden, pair, back, 2 * xs)
    my_rows, gram = rows_and_gram(me, exchanged(pieces, COL), own, 1.0 / total_rows)
    count = 4 * xs
    gram = total(exchanged(gram.reshape(count, 3 * HALF // count, HALF), NEAR))
    gram = total(exchanged(spread(gram, zs), "z"))
    gram = total(exchanged(spread(gram, ys // 2), "y_hi"))
    gram = exchanged(spread(gram, count), NEAR).reshape(3 * HALF, HALF)
    return factor_call(gram, my_rows)


def solution(mesh):
    rows, cols = mesh.devices.shape
    side = math.isqrt(rows)
    sizes = (side, rows // side, cols // 2)
    grid = Mesh(mesh.devices.reshape(side // 2, 2, *sizes[1:], 2), ALL)
    in_specs = (P(ROW, COL), P(COL, None))
    out_specs = (P(ALL, None), P())
    return jax.shard_map(
        lambda *args: body(sizes, *args), mesh=grid, in_specs=in_specs, out_specs=out_specs, check_vma=False
    )
```

```python
import math

import jax
import jax.numpy as jnp
from jax import lax
from jax.experimental import pallas as pl
from jax.experimental.pallas import tpu as pltpu
from jax.sharding import Mesh, PartitionSpec as P

D = 7168
K = 256
HALF = K // 2
HIGH = lax.Precision.HIGHEST

def dot(a, b, over_a=1, over_b=0, precision=None):
    return lax.dot_general(
        a, b, (((over_a,), (over_b,)), ((), ())), precision=precision, preferred_element_type=jnp.float32
    )


def terms(a):
    high = a.astype(jnp.bfloat16)
    return high, (a - high.astype(jnp.float32)).astype(jnp.bfloat16)


def factor_kernel(packed_ref, rows_ref, basis_ref, factor_ref, gram_ref, g_ref, x_ref, work_ref):
    bf16 = jnp.bfloat16
    corner = packed_ref[HALF : 2 * HALF, :]
    gram_ref[:HALF, :HALF] = packed_ref[:HALF, :]
    gram_ref[:HALF, HALF:] = corner
    gram_ref[HALF:, :HALF] = corner.T
    gram_ref[HALF:, HALF:] = packed_ref[2 * HALF :, :]
    row = lax.broadcasted_iota(jnp.int32, (K, K), 0)
    col = lax.broadcasted_iota(jnp.int32, (K, K), 1)
    eye = (row == col).astype(jnp.float32)
    upper = jnp.where(row < col, 1.0, jnp.where(row == col, 0.5, 0.0))
    on_diag = jnp.where(row == col, gram_ref[...], 0.0)
    s_row = lax.rsqrt(jnp.sum(on_diag, axis=0, keepdims=True))
    s_col = lax.rsqrt(jnp.sum(on_diag, axis=1, keepdims=True))

    def change_for(g):
        f = (g - eye) * upper
        fb = f.astype(bf16)
        a = f - dot(fb, fb, 0, 0) * upper
        ab = a.astype(bf16)
        return (dot(ab, ab) - a).astype(bf16)

    def moved(g, n):
        y = g + sum(dot(part, n) for part in terms(g))
        return y + sum(dot(n, part, 0, 0) for part in terms(y))

    def size(e):
        return jnp.sum(e * e)

    g = gram_ref[...] * s_row * s_col
    n = change_for(g)
    x_ref[...] = s_col * (eye + n.astype(jnp.float32))
    g_ref[...] = moved(g, n)

    def step(state):
        count, _ = state
        g = g_ref[...]
        n = change_for(g)
        g = moved(g, n)
        g_ref[...] = g
        x = x_ref[...]
        x_ref[...] = x + sum(dot(part, n) for part in terms(x))
        return count + 1, size(g - eye)

    def more(state):
        count, err = state
        return jnp.logical_and(count < 12, err > 1e-5)

    _, err = lax.while_loop(more, step, (jnp.int32(0), jnp.float32(1.0)))
    ok = err <= 1e-5

    @pl.when(ok)
    def _():
        x = x_ref[...]
        last = ((g_ref[...] - eye) * upper).astype(bf16)
        x_ref[...] = x - dot(x.astype(bf16), last)

    @pl.when(jnp.logical_not(ok))
    def _():
        work_ref[:, :K] = gram_ref[...]
        work_ref[:, K:] = eye
        lane = lax.broadcasted_iota(jnp.int32, (1, 2 * K), 1)

        def eliminate(k, carry):
            line = work_ref[pl.ds(k, 1), :]
            pivot = jnp.sum(jnp.where(lane == k, line, 0.0), axis=1, keepdims=True)
            scale = lax.rsqrt(pivot)
            line = line * (scale * (1.5 - 0.5 * pivot * scale * scale))
            coef = jnp.where(lane[:, :K] > k, line[:, :K], 0.0)
            work_ref[...] = work_ref[...] - dot(coef, line, 0, 0, HIGH)
            work_ref[pl.ds(k, 1), :] = line
            return carry

        lax.fori_loop(0, K, eliminate, 0)
        x_ref[...] = work_ref[:, K:].T

    x = jnp.where(row <= col, x_ref[...], 0.0)
    basis_ref[...] = dot(rows_ref[...], x, precision=HIGH)
    factor_ref[...] = jnp.where(row <= col, dot(x, gram_ref[...], 0, 0, HIGH), 0.0)


def factor_call(packed, rows):
    square = pltpu.VMEM((K, K), jnp.float32)
    return pl.pallas_call(
        factor_kernel,
        out_shape=(jax.ShapeDtypeStruct(rows.shape, jnp.float32), jax.ShapeDtypeStruct((K, K), jnp.float32)),
        in_specs=[WHOLE] * 2,
        out_specs=(WHOLE, WHOLE),
        scratch_shapes=[square, square, square, pltpu.VMEM((K, 2 * K), jnp.float32)],
        compiler_params=PARAMS,
        name="factor",
    )(packed, rows)


WHOLE = pl.BlockSpec(memory_space=pltpu.VMEM)
PARAMS = pltpu.CompilerParams(vmem_limit_bytes=12 * 1024 * 1024)


SCALAR = pl.BlockSpec(memory_space=pltpu.SMEM)
STEPS = 8


def half_columns(core_ref):
    return pl.ds(pl.multiple_of(core_ref[0] * HALF, HALF), HALF)


def opening_kernel(core_ref, hidden_ref, right_ref, first_ref, hidden_out, right_buf, sems):
    rows = hidden_out.shape[0] // STEPS
    blocks = [slice(i * rows, (i + 1) * rows) for i in range(STEPS)]
    copies = [pltpu.make_async_copy(right_ref, right_buf, sems.at[STEPS])]
    for i, block in enumerate(blocks):
        copies.append(pltpu.make_async_copy(hidden_ref.at[block, :], hidden_out.at[block, :], sems.at[i]))
    for copy in copies:
        copy.start()
    for copy in copies:
        copy.wait()
    first_ref[...] = dot(hidden_out[...], right_buf[:, half_columns(core_ref)])


def opening(core, hidden, right):
    in_hbm = pl.BlockSpec(memory_space=pltpu.HBM)
    return pl.pallas_call(
        opening_kernel,
        out_shape=(
            jax.ShapeDtypeStruct((hidden.shape[0], HALF), jnp.float32),
            jax.ShapeDtypeStruct(hidden.shape, hidden.dtype),
        ),
        in_specs=[SCALAR, in_hbm, in_hbm],
        out_specs=(WHOLE, WHOLE),
        scratch_shapes=[pltpu.VMEM(right.shape, right.dtype), pltpu.SemaphoreType.DMA((STEPS + 1,))],
        compiler_params=PARAMS,
        name="opening",
    )(
        core,
        pltpu.with_memory_space_constraint(hidden, pltpu.HBM),
        pltpu.with_memory_space_constraint(right, pltpu.HBM),
    )


def pieces_kernel(core_ref, own_ref, pair_ref, right_ref, pieces_ref):
    count, tile, _ = pieces_ref.shape
    first = own_ref[...] + dot(pair_ref[...], right_ref[:, half_columns(core_ref)])
    for i in range(count):
        pieces_ref[i] = first[i * tile : (i + 1) * tile, :].astype(pieces_ref.dtype)


def first_pieces(core, own, pair, right, count):
    return pl.pallas_call(
        pieces_kernel,
        out_shape=jax.ShapeDtypeStruct((count, own.shape[0] // count, HALF), jnp.bfloat16),
        in_specs=[SCALAR, WHOLE, WHOLE, WHOLE],
        out_specs=WHOLE,
        compiler_params=PARAMS,
        name="first_pieces",
    )(core, own, pair, right)


def back_kernel(first_ref, own_ref, pair_ref, out_ref):
    first = first_ref[...]
    out_ref[:HALF, :] = dot(first, own_ref[...], 0, 0).astype(out_ref.dtype)
    out_ref[HALF:, :] = dot(first, pair_ref[...], 0, 0).astype(out_ref.dtype)


def local_backs(first, own, pair):
    return pl.pallas_call(
        back_kernel,
        out_shape=jax.ShapeDtypeStruct((K, own.shape[1]), jnp.bfloat16),
        in_specs=[WHOLE] * 3,
        out_specs=WHOLE,
        compiler_params=PARAMS,
        name="local_backs",
    )(first, own, pair)


def sketch_kernel(own_ref, pair_ref, back_ref, out_ref):
    out_ref[...] = dot(own_ref[...], back_ref[:HALF, :], 1, 1) + dot(pair_ref[...], back_ref[HALF:, :], 1, 1)


def partial_sketch(own, pair, back):
    return pl.pallas_call(
        sketch_kernel,
        out_shape=jax.ShapeDtypeStruct((own.shape[0], HALF), jnp.float32),
        in_specs=[WHOLE] * 3,
        out_specs=WHOLE,
        compiler_params=PARAMS,
        name="partial_sketch",
    )(own, pair, back)


def gram_kernel(scale, landed_ref, rows_ref, packed_ref):
    halves = []
    for half in range(2):
        parts = [landed_ref[i] for i in range(half, landed_ref.shape[0], 2)]
        halves.append(sum(parts[1:], parts[0]))
    left, right = halves
    rows_ref[:, :HALF] = left
    rows_ref[:, HALF:] = right
    packed_ref[:HALF, :] = dot(left, left, 0, 0, HIGH) * scale
    packed_ref[HALF : 2 * HALF, :] = dot(left, right, 0, 0, HIGH) * scale
    packed_ref[2 * HALF :, :] = dot(right, right, 0, 0, HIGH) * scale


def rows_and_gram(landed, scale):
    return pl.pallas_call(
        lambda *refs: gram_kernel(scale, *refs),
        out_shape=(
            jax.ShapeDtypeStruct((landed.shape[1], K), jnp.float32),
            jax.ShapeDtypeStruct((3 * HALF, HALF), jnp.float32),
        ),
        in_specs=[WHOLE],
        out_specs=(WHOLE, WHOLE),
        compiler_params=PARAMS,
        name="rows_and_gram",
    )(landed)


ROW = ("y_hi", "y_lo", "z")
COL = ("x", "core")
NEAR = ("y_lo", *COL)
ALL = (*ROW, *COL)


def swapped(block):
    return lax.ppermute(block, "core", [(0, 1), (1, 0)])


def line_groups(sizes, along):
    ys, zs, xs = sizes
    groups = []
    for core in range(2):
        y_steps, z_steps = along[core]
        for y in range(ys):
            for z in range(zs):
                if any(y // s % n for s, n in y_steps) or any(z // s % n for s, n in z_steps):
                    continue
                spots = [(y, z)]
                for s, n in y_steps:
                    spots = [(a + s * k, b) for a, b in spots for k in range(n)]
                for s, n in z_steps:
                    spots = [(a, b + s * k) for a, b in spots for k in range(n)]
                for x in range(xs):
                    groups.append([((a * zs + b) * xs + x) * 2 + core for a, b in spots])
    return groups


def exchanged(pieces, axis, groups=None):
    return lax.all_to_all(pieces, axis, 0, 0, axis_index_groups=groups)


def spread(block, count):
    return jnp.broadcast_to(block[None], (count, *block.shape))


def total(pieces):
    return jnp.sum(pieces.astype(jnp.float32), axis=0)


def body(sizes, hidden, test_matrix):
    bf16 = jnp.bfloat16
    tok_rows, width = hidden.shape
    ys, zs, xs = sizes
    total_rows = tok_rows * ys * zs
    core = lax.axis_index("core").reshape(1)

    pair, right = swapped(hidden), swapped(test_matrix)
    own, hidden = opening(core, hidden, test_matrix)
    pieces = first_pieces(core, own, pair, right, xs)
    first = (total(exchanged(pieces, "x")) * (1.0 / math.sqrt(D))).astype(bf16)
    first = exchanged(spread(first, xs), "x").reshape(tok_rows, HALF)
    local_back = local_backs(first, hidden, pair)

    lines = ((), ((1, zs),)), (((1, ys),), ())
    this_way, that_way = line_groups(sizes, lines), line_groups(sizes, lines[::-1])
    count = len(this_way[0])
    pieces = local_back.reshape(count, K // count, width)
    my_back = total(exchanged(pieces, ALL, this_way)).astype(bf16)
    my_back = total(exchanged(spread(my_back, len(that_way[0])), ALL, that_way))
    my_back = (my_back * (1.0 / total_rows)).astype(bf16)
    back = exchanged(spread(my_back, count), ALL, this_way).reshape(K, width)

    pieces = partial_sketch(hidden, pair, back).reshape(2 * xs, tok_rows // (2 * xs), HALF)
    my_rows, gram = rows_and_gram(exchanged(pieces, COL), 1.0 / total_rows)
    count = 4 * xs
    gram = total(exchanged(gram.reshape(count, 3 * HALF // count, HALF), NEAR))
    gram = total(exchanged(spread(gram, zs), "z"))
    gram = total(exchanged(spread(gram, ys // 2), "y_hi"))
    gram = exchanged(spread(gram, count), NEAR).reshape(3 * HALF, HALF)
    return factor_call(gram, my_rows)


def solution(mesh):
    rows, cols = mesh.devices.shape
    side = math.isqrt(rows)
    sizes = (side, rows // side, cols // 2)
    grid = Mesh(mesh.devices.reshape(side // 2, 2, *sizes[1:], 2), ALL)
    in_specs = (P(ROW, COL), P(COL, None))
    out_specs = (P(ALL, None), P())
    return jax.shard_map(
        lambda *args: body(sizes, *args), mesh=grid, in_specs=in_specs, out_specs=out_specs, check_vma=False
    )
```

```python
import math

import jax
import jax.numpy as jnp
from jax import lax
from jax.experimental import pallas as pl
from jax.experimental.pallas import tpu as pltpu
from jax.sharding import Mesh, PartitionSpec as P

D = 7168
K = 256
HALF = K // 2
HIGH = lax.Precision.HIGHEST

def dot(a, b, over_a=1, over_b=0, precision=None):
    return lax.dot_general(
        a, b, (((over_a,), (over_b,)), ((), ())), precision=precision, preferred_element_type=jnp.float32
    )


def terms(a):
    high = a.astype(jnp.bfloat16)
    return high, (a - high.astype(jnp.float32)).astype(jnp.bfloat16)


def factor_kernel(packed_ref, rows_ref, basis_ref, factor_ref, gram_ref, g_ref, x_ref, work_ref):
    bf16 = jnp.bfloat16
    corner = packed_ref[HALF : 2 * HALF, :]
    gram_ref[:HALF, :HALF] = packed_ref[:HALF, :]
    gram_ref[:HALF, HALF:] = corner
    gram_ref[HALF:, :HALF] = corner.T
    gram_ref[HALF:, HALF:] = packed_ref[2 * HALF :, :]
    row = lax.broadcasted_iota(jnp.int32, (K, K), 0)
    col = lax.broadcasted_iota(jnp.int32, (K, K), 1)
    eye = (row == col).astype(jnp.float32)
    upper = jnp.where(row < col, 1.0, jnp.where(row == col, 0.5, 0.0))
    on_diag = jnp.where(row == col, gram_ref[...], 0.0)
    s_row = lax.rsqrt(jnp.sum(on_diag, axis=0, keepdims=True))
    s_col = lax.rsqrt(jnp.sum(on_diag, axis=1, keepdims=True))

    def change_for(g):
        f = (g - eye) * upper
        fb = f.astype(bf16)
        a = f - dot(fb, fb, 0, 0) * upper
        ab = a.astype(bf16)
        return (dot(ab, ab) - a).astype(bf16)

    def moved(g, n):
        y = g + sum(dot(part, n) for part in terms(g))
        return y + sum(dot(n, part, 0, 0) for part in terms(y))

    def size(e):
        return jnp.sum(e * e)

    g = gram_ref[...] * s_row * s_col
    n = change_for(g)
    x_ref[...] = s_col * (eye + n.astype(jnp.float32))
    g_ref[...] = moved(g, n)

    def step(state):
        count, _ = state
        g = g_ref[...]
        n = change_for(g)
        g = moved(g, n)
        g_ref[...] = g
        x = x_ref[...]
        x_ref[...] = x + sum(dot(part, n) for part in terms(x))
        return count + 1, size(g - eye)

    def more(state):
        count, err = state
        return jnp.logical_and(count < 12, err > 1e-5)

    _, err = lax.while_loop(more, step, (jnp.int32(0), jnp.float32(1.0)))
    ok = err <= 1e-5

    @pl.when(ok)
    def _():
        x = x_ref[...]
        last = ((g_ref[...] - eye) * upper).astype(bf16)
        x = jnp.where(row <= col, x - dot(x.astype(bf16), last), 0.0)
        (x_high, x_low), (r_high, r_low), (g_high, g_low) = terms(x), terms(rows_ref[...]), terms(gram_ref[...])
        basis_ref[...] = dot(r_high, x_high) + (dot(r_high, x_low) + dot(r_low, x_high))
        factor = dot(x_high, g_high, 0) + (dot(x_high, g_low, 0) + dot(x_low, g_high, 0))
        factor_ref[...] = jnp.where(row <= col, factor, 0.0)

    @pl.when(jnp.logical_not(ok))
    def _():
        work_ref[:, :K] = gram_ref[...]
        work_ref[:, K:] = eye
        lane = lax.broadcasted_iota(jnp.int32, (1, 2 * K), 1)

        def eliminate(k, carry):
            line = work_ref[pl.ds(k, 1), :]
            pivot = jnp.sum(jnp.where(lane == k, line, 0.0), axis=1, keepdims=True)
            scale = lax.rsqrt(pivot)
            line = line * (scale * (1.5 - 0.5 * pivot * scale * scale))
            coef = jnp.where(lane[:, :K] > k, line[:, :K], 0.0)
            work_ref[...] = work_ref[...] - dot(coef, line, 0, 0, HIGH)
            work_ref[pl.ds(k, 1), :] = line
            return carry

        lax.fori_loop(0, K, eliminate, 0)
        x = jnp.where(row <= col, work_ref[:, K:].T, 0.0)
        basis_ref[...] = dot(rows_ref[...], x, precision=HIGH)
        factor_ref[...] = jnp.where(row <= col, work_ref[:, :K], 0.0)


def factor_call(packed, rows):
    square = pltpu.VMEM((K, K), jnp.float32)
    return pl.pallas_call(
        factor_kernel,
        out_shape=(jax.ShapeDtypeStruct(rows.shape, jnp.float32), jax.ShapeDtypeStruct((K, K), jnp.float32)),
        in_specs=[WHOLE] * 2,
        out_specs=(WHOLE, WHOLE),
        scratch_shapes=[square, square, square, pltpu.VMEM((K, 2 * K), jnp.float32)],
        compiler_params=PARAMS,
        name="factor",
    )(packed, rows)


WHOLE = pl.BlockSpec(memory_space=pltpu.VMEM)
PARAMS = pltpu.CompilerParams(vmem_limit_bytes=12 * 1024 * 1024)


SCALAR = pl.BlockSpec(memory_space=pltpu.SMEM)
STEPS = 8


def half_columns(core_ref):
    return pl.ds(pl.multiple_of(core_ref[0] * HALF, HALF), HALF)


def opening_kernel(core_ref, me_ref, hidden_ref, right_ref, first_ref, hidden_out, right_buf, sems):
    rows = hidden_out.shape[0] // STEPS
    blocks = [slice(i * rows, (i + 1) * rows) for i in range(STEPS)]
    copies = [pltpu.make_async_copy(right_ref, right_buf, sems.at[STEPS])]
    for i, block in enumerate(blocks):
        copies.append(pltpu.make_async_copy(hidden_ref.at[block, :], hidden_out.at[block, :], sems.at[i]))
    for copy in copies:
        copy.start()
    for copy in copies:
        copy.wait()
    first_ref[...] = dot(hidden_out[...], right_buf[:, half_columns(core_ref)])


def opening(core, me, hidden, right):
    in_hbm = pl.BlockSpec(memory_space=pltpu.HBM)
    return pl.pallas_call(
        opening_kernel,
        out_shape=(
            jax.ShapeDtypeStruct((hidden.shape[0], HALF), jnp.float32),
            jax.ShapeDtypeStruct(hidden.shape, hidden.dtype),
        ),
        in_specs=[SCALAR, SCALAR, in_hbm, in_hbm],
        out_specs=(WHOLE, WHOLE),
        scratch_shapes=[pltpu.VMEM(right.shape, right.dtype), pltpu.SemaphoreType.DMA((STEPS + 1,))],
        compiler_params=PARAMS,
        name="opening",
    )(
        core,
        me,
        pltpu.with_memory_space_constraint(hidden, pltpu.HBM),
        pltpu.with_memory_space_constraint(right, pltpu.HBM),
    )


def pieces_kernel(core_ref, own_ref, pair_ref, right_ref, pieces_ref):
    count, tile, _ = pieces_ref.shape
    first = own_ref[...] + dot(pair_ref[...], right_ref[:, half_columns(core_ref)])
    for i in range(count):
        pieces_ref[i] = first[i * tile : (i + 1) * tile, :].astype(pieces_ref.dtype)


def first_pieces(core, own, pair, right, count):
    return pl.pallas_call(
        pieces_kernel,
        out_shape=jax.ShapeDtypeStruct((count, own.shape[0] // count, HALF), jnp.bfloat16),
        in_specs=[SCALAR, WHOLE, WHOLE, WHOLE],
        out_specs=WHOLE,
        compiler_params=PARAMS,
        name="first_pieces",
    )(core, own, pair, right)


def back_kernel(first_ref, own_ref, pair_ref, out_ref):
    first = first_ref[...]
    out_ref[:HALF, :] = dot(first, own_ref[...], 0, 0).astype(out_ref.dtype)
    out_ref[HALF:, :] = dot(first, pair_ref[...], 0, 0).astype(out_ref.dtype)


def local_backs(first, own, pair):
    return pl.pallas_call(
        back_kernel,
        out_shape=jax.ShapeDtypeStruct((K, own.shape[1]), jnp.bfloat16),
        in_specs=[WHOLE] * 3,
        out_specs=WHOLE,
        compiler_params=PARAMS,
        name="local_backs",
    )(first, own, pair)


def sketch_kernel(me_ref, own_ref, pair_ref, back_ref, mine_ref, pieces_ref):
    count, tile, _ = pieces_ref.shape
    sketch = dot(own_ref[...], back_ref[:HALF, :], 1, 1) + dot(pair_ref[...], back_ref[HALF:, :], 1, 1)
    for i in range(count):
        block = sketch[i * tile : (i + 1) * tile, :]
        pieces_ref[i] = block.astype(pieces_ref.dtype)

        @pl.when(me_ref[0] == i)
        def _():
            mine_ref[...] = block


def sketch_pieces(me, own, pair, back, count):
    tile = own.shape[0] // count
    return pl.pallas_call(
        sketch_kernel,
        out_shape=(
            jax.ShapeDtypeStruct((tile, HALF), jnp.float32),
            jax.ShapeDtypeStruct((count, tile, HALF), jnp.bfloat16),
        ),
        in_specs=[SCALAR, WHOLE, WHOLE, WHOLE],
        out_specs=(WHOLE, WHOLE),
        compiler_params=PARAMS,
        name="sketch_pieces",
    )(me, own, pair, back)


def gram_kernel(scale, me_ref, landed_ref, own_ref, rows_ref, packed_ref):
    halves = []
    for half in range(2):
        parts = [
            jnp.where(me_ref[0] == i, own_ref[...], landed_ref[i].astype(jnp.float32))
            for i in range(half, landed_ref.shape[0], 2)
        ]
        halves.append(sum(parts[1:], parts[0]))
    left, right = halves
    rows_ref[:, :HALF] = left
    rows_ref[:, HALF:] = right
    packed_ref[:HALF, :] = dot(left, left, 0, 0, HIGH) * scale
    packed_ref[HALF : 2 * HALF, :] = dot(left, right, 0, 0, HIGH) * scale
    packed_ref[2 * HALF :, :] = dot(right, right, 0, 0, HIGH) * scale


def rows_and_gram(me, landed, own, scale):
    return pl.pallas_call(
        lambda *refs: gram_kernel(scale, *refs),
        out_shape=(
            jax.ShapeDtypeStruct((own.shape[0], K), jnp.float32),
            jax.ShapeDtypeStruct((3 * HALF, HALF), jnp.float32),
        ),
        in_specs=[SCALAR, WHOLE, WHOLE],
        out_specs=(WHOLE, WHOLE),
        compiler_params=PARAMS,
        name="rows_and_gram",
    )(me, landed, own)


ROW = ("y_hi", "y_lo", "z")
COL = ("x", "core")
NEAR = ("y_lo", *COL)
ALL = (*ROW, *COL)


def swapped(block):
    return lax.ppermute(block, "core", [(0, 1), (1, 0)])


def line_groups(sizes, along):
    ys, zs, xs = sizes
    groups = []
    for core in range(2):
        y_steps, z_steps = along[core]
        for y in range(ys):
            for z in range(zs):
                if any(y // s % n for s, n in y_steps) or any(z // s % n for s, n in z_steps):
                    continue
                spots = [(y, z)]
                for s, n in y_steps:
                    spots = [(a + s * k, b) for a, b in spots for k in range(n)]
                for s, n in z_steps:
                    spots = [(a, b + s * k) for a, b in spots for k in range(n)]
                for x in range(xs):
                    groups.append([((a * zs + b) * xs + x) * 2 + core for a, b in spots])
    return groups


def exchanged(pieces, axis, groups=None):
    return lax.all_to_all(pieces, axis, 0, 0, axis_index_groups=groups)


def spread(block, count):
    return jnp.broadcast_to(block[None], (count, *block.shape))


def total(pieces):
    return jnp.sum(pieces.astype(jnp.float32), axis=0)


def body(sizes, hidden, test_matrix):
    bf16 = jnp.bfloat16
    tok_rows, width = hidden.shape
    ys, zs, xs = sizes
    total_rows = tok_rows * ys * zs
    core, me = (lax.axis_index(axis).reshape(1) for axis in ("core", COL))

    pair, right = swapped(hidden), swapped(test_matrix)
    own, hidden = opening(core, me, hidden, test_matrix)
    pieces = first_pieces(core, own, pair, right, xs)
    first = (total(exchanged(pieces, "x")) * (1.0 / math.sqrt(D))).astype(bf16)
    first = exchanged(spread(first, xs), "x").reshape(tok_rows, HALF)
    local_back = local_backs(first, hidden, pair)

    lines = ((), ((1, zs),)), (((1, ys),), ())
    this_way, that_way = line_groups(sizes, lines), line_groups(sizes, lines[::-1])
    count = len(this_way[0])
    pieces = local_back.reshape(count, K // count, width)
    my_back = total(exchanged(pieces, ALL, this_way)).astype(bf16)
    my_back = total(exchanged(spread(my_back, len(that_way[0])), ALL, that_way))
    my_back = (my_back * (1.0 / total_rows)).astype(bf16)
    back = exchanged(spread(my_back, count), ALL, this_way).reshape(K, width)

    own, pieces = sketch_pieces(me, hidden, pair, back, 2 * xs)
    my_rows, gram = rows_and_gram(me, exchanged(pieces, COL), own, 1.0 / total_rows)
    count = 4 * xs
    gram = total(exchanged(gram.reshape(count, 3 * HALF // count, HALF), NEAR))
    gram = total(exchanged(spread(gram, zs), "z"))
    gram = total(exchanged(spread(gram, ys // 2), "y_hi"))
    gram = exchanged(spread(gram, count), NEAR).reshape(3 * HALF, HALF)
    return factor_call(gram, my_rows)


def solution(mesh):
    rows, cols = mesh.devices.shape
    side = math.isqrt(rows)
    sizes = (side, rows // side, cols // 2)
    grid = Mesh(mesh.devices.reshape(side // 2, 2, *sizes[1:], 2), ALL)
    in_specs = (P(ROW, COL), P(COL, None))
    out_specs = (P(ALL, None), P())
    return jax.shard_map(
        lambda *args: body(sizes, *args), mesh=grid, in_specs=in_specs, out_specs=out_specs, check_vma=False
    )
```
